256 devices in a mesh: slot: 32 (over x, z), tp: 8 (over y, core).
Axes of the slice: x: 4, y: 4, z: 8, core: 2. Of those that a mesh axis runs over, the one named last changes fastest.
Arguments:
- queries: bfloat16 [8192, 6144], P('slot', 'tp'), may hold values from -150 to 150
- k_new: bfloat16 [8192, 6144], P('slot', 'tp'), may hold values from -7 to 7
- v_new: bfloat16 [8192, 6144], P('slot', 'tp'), may hold values from -6 to 6
- k_clean: bfloat16 [8192, 6144], P('slot', 'tp'), may hold values from -6 to 6
- v_clean: bfloat16 [8192, 6144], P('slot', 'tp'), may hold values from -6 to 6
- lists: int32 [32, 62], replicated, may hold values from 0 to 495, as said below
- counts: int32 [32], replicated, may hold values from 0 to 62, as said below
- resid: bfloat16 [8192, 6144], P('slot', 'tp'), may hold values from -1.5 to 1.5
- w_out: bfloat16 [6144, 6144], P('tp', 'slot'), may hold values from -0.29882812 to 0.29882812
Outputs:
- layer_out: bfloat16 [8192, 6144], P('slot', 'tp')
The draws below stay inside these ranges and needn't reach their ends.
Inputs may be any that keep to these rules, and one draw needn't show every extreme that they name: Row c lists only blocks of groups before c, no block twice, at most 2 blocks of one group and exactly 2 of group c-1, in group order; entries from counts[c] on are 0 and unused. counts[c] lies between c and 2 * c; the last group reads exactly 2 blocks of every earlier group.
All inputs are finite; a program needn't handle non-finite values.
Results may differ from the reference program's by a relative error of at most 0.02.
Values may be sent and summed in bfloat16 or wider, within the bound.
A program may use at most 192 MiB of HBM per device.

```python
import math
import jax
import jax.numpy as jnp
from jax import lax

D = 6144
HEADS = 48
HEAD_DIM = 128
TOK_DEV = 256
BLK = 16
CAP = 2
TOKENS = 8192
NBLK = 512
MAXR = 62


def shared_base(key):
    return jnp.clip(jax.random.normal(key, (TOKENS, D), jnp.float32), -6.0, 6.0)


def draw_k_new(key, part):
    base = shared_base(key)
    return base.astype(jnp.bfloat16)


def draw_queries(key, part):
    key = jax.random.fold_in(key, 12)
    drawn = jnp.clip(jax.random.normal(key, (TOKENS, D), jnp.float32), -6.0, 6.0)
    return drawn.astype(jnp.bfloat16)


def route_tables(key):
    slots = TOKENS // TOK_DEV
    per = TOK_DEV // BLK
    keys = jax.random.split(jax.random.fold_in(key, 5), slots * slots)
    perms = jax.vmap(lambda k: jax.random.permutation(k, per))(keys).reshape(slots, slots, per)
    take = jax.random.randint(jax.random.fold_in(key, 6), (slots, slots), 1, CAP + 1)
    reader = jnp.arange(slots)[:, None]
    owner = jnp.arange(slots)[None, :]
    take = jnp.where(owner == reader - 1, CAP, take)
    take = jnp.where(reader == slots - 1, CAP, take)
    pair = (reader == slots - 1) & (owner == slots - 2)
    shifted = (perms - perms[:, :, :1] + per - 1) % per
    perms = jnp.where(pair[:, :, None], shifted, perms)
    within = jnp.arange(CAP)
    valid = (owner < reader)[:, :, None] & (within[None, None, :] < take[:, :, None])
    ids = (owner[:, :, None] * per + perms[:, :, :CAP]).astype(jnp.int32)
    flatv = valid.reshape(slots, slots * CAP)
    flati = ids.reshape(slots, slots * CAP)
    pos = jnp.cumsum(flatv.astype(jnp.int32), 1) - 1
    pos = jnp.where(flatv, pos, MAXR)
    table = jnp.zeros((slots, MAXR + 1), jnp.int32).at[jnp.arange(slots)[:, None], pos].set(flati)
    return (table[:, :MAXR], jnp.sum(flatv.astype(jnp.int32), 1))


def draw_lists(key, part):
    table, total = route_tables(key)
    return table


def draw_counts(key, part):
    table, total = route_tables(key)
    return total


def block_scale(key, shape, cuts, least, largest):
    loudness, own = 1.0, jax.random.fold_in(key, 6)
    for dim, blocks in cuts:
        heights = jnp.exp(jax.random.uniform(jax.random.fold_in(own, dim), (blocks,), jnp.float32, least / len(cuts), largest / len(cuts)))
        loudness = loudness * jnp.repeat(heights, shape[dim] // blocks).reshape([-1 if axis == dim else 1 for axis in range(len(shape))])
    return loudness


def centred(key, extent, scale, limit, cuts=(), kind=jnp.bfloat16):
    values = jax.random.normal(key, extent, jnp.float32) * scale
    if len(cuts) > 0:
        values = block_scale(key, extent, cuts, -0.22, 0.18) * values
    return jnp.clip(values, min=-limit, max=limit).astype(kind)


def setup_inputs(seed: int = 0) -> dict:
    streams_of = jax.random.split(jax.random.key(seed), 10)
    return {
        "queries": draw_queries(jax.random.fold_in(streams_of[9], 71), 0),
        "k_new": draw_k_new(jax.random.fold_in(streams_of[9], 71), 0),
        "v_new": centred(streams_of[2], (TOKENS, D), 1.0, 6.0, ((0, 32), (1, 8))),
        "k_clean": centred(streams_of[3], (TOKENS, D), 1.0, 6.0, ((0, 32), (1, 8))),
        "v_clean": centred(streams_of[4], (TOKENS, D), 1.0, 6.0, ((0, 32), (1, 8))),
        "lists": draw_lists(jax.random.fold_in(streams_of[9], 71), 0),
        "counts": draw_counts(jax.random.fold_in(streams_of[9], 71), 0),
        "resid": centred(streams_of[7], (TOKENS, D), 0.25, 1.5, ((0, 32), (1, 8))),
        "w_out": centred(streams_of[8], (D, D), 0.05, 0.29882812, ((0, 8), (1, 32))),
    }


def reference(queries, k_new, v_new, k_clean, v_clean, lists, counts, resid, w_out):
    slots = TOKENS // TOK_DEV
    scale = 1.0 / math.sqrt(HEAD_DIM)
    kb = k_clean.reshape(NBLK, BLK, D)
    vb = v_clean.reshape(NBLK, BLK, D)

    def one(s):
        s = s.astype(jnp.int32)
        q = lax.dynamic_slice_in_dim(queries, s * TOK_DEV, TOK_DEV, 0).astype(jnp.float32)
        ko = lax.dynamic_slice_in_dim(k_new, s * TOK_DEV, TOK_DEV, 0)
        vo = lax.dynamic_slice_in_dim(v_new, s * TOK_DEV, TOK_DEV, 0)
        ids = lists[s]
        live = jnp.arange(MAXR, dtype=jnp.int32) < counts[s]
        keys = jnp.concatenate([ko, kb[ids].reshape(MAXR * BLK, D)], 0).astype(jnp.float32)
        vals = jnp.concatenate([vo, vb[ids].reshape(MAXR * BLK, D)], 0).astype(jnp.float32)
        allowed = jnp.concatenate([jnp.ones((TOK_DEV,), bool), jnp.repeat(live, BLK)], 0)
        q3 = q.reshape(TOK_DEV, HEADS, HEAD_DIM)
        k3 = keys.reshape(-1, HEADS, HEAD_DIM)
        v3 = vals.reshape(-1, HEADS, HEAD_DIM)
        sc = jnp.einsum('qhd,khd->hqk', q3, k3, precision=lax.Precision.HIGHEST) * scale
        sc = jnp.where(allowed[None, None, :], sc, -jnp.inf)
        top = lax.optimization_barrier(jnp.max(sc, -1, keepdims=True))
        ex = jnp.exp(sc - top)
        total = lax.optimization_barrier(jnp.sum(ex, -1))
        probs = lax.optimization_barrier(ex.astype(jnp.bfloat16)).astype(jnp.float32)
        out = jnp.einsum('hqk,khd->hqd', probs, v3, precision=lax.Precision.HIGHEST)
        out = out / total[..., None]
        return jnp.transpose(out, (1, 0, 2)).reshape(TOK_DEV, D).astype(jnp.bfloat16)
    attn = lax.map(one, jnp.arange(slots, dtype=jnp.int32)).reshape(TOKENS, D)
    proj = jnp.dot(attn, w_out, preferred_element_type=jnp.float32)
    return (resid.astype(jnp.float32) + proj).astype(jnp.bfloat16)
```

```python
import math

import jax
import jax.numpy as jnp
from jax import lax
from jax.experimental import pallas as pl
from jax.experimental.pallas import tpu as pltpu
from jax.sharding import PartitionSpec as P

HD = 128
BLK = 16
NX, NZ, NY = 4, 8, 4
RING = (1, 7, 2, 6, 3, 5, 4)
MESH = pl.DeviceIdType.MESH
BF = jnp.bfloat16
F32 = jnp.float32
NEG = -1e30
NT = (((1,), (1,)), ((), ()))
VM = pltpu.VMEM
DMA = pltpu.SemaphoreType.DMA


def remote(src, dst, ssem, rsem, **where):
    return pltpu.make_async_remote_copy(
        src_ref=src, dst_ref=dst, send_sem=ssem, recv_sem=rsem, device_id=where, device_id_type=MESH
    )


def loop(lo, hi, body):
    def step(i, c):
        body(i)
        return c

    lax.fori_loop(lo, hi, step, 0)


def attention_kernel(
    q, kn, vn, kc, vc, wt, lists, counts,
    attn, wall,
    sk, sv, kb, vb, rk, rv, wz, hot, seen, mx, tot, acc,
    k1s, k1r, k2s, k2r, v1s, v1r, v2s, v2r, os, orr, w1s, w1r, wps, wpr, wms, wmr, wcs, wcr,
):
    me = lax.axis_index("slot")
    tp = lax.axis_index("tp")
    x, z, core = me // NZ, me % NZ, tp % 2
    sib = tp + 1 - 2 * core
    heads = q.shape[1] // HD
    c2 = math.log2(math.e) / math.sqrt(HD)

    def at(ax, az):
        return ax * NZ + az

    barrier = pltpu.get_barrier_semaphore()
    for d in range(1, NX):
        pl.semaphore_signal(barrier, inc=1, device_id={"slot": at((x + d) % NX, z)}, device_id_type=MESH)
    for d in range(1, NZ):
        pl.semaphore_signal(barrier, inc=1, device_id={"slot": at(x, (z + d) % NZ)}, device_id_type=MESH)
    pl.semaphore_signal(barrier, inc=1, device_id={"tp": sib}, device_id_type=MESH)

    lst = lists[...]
    live = lax.broadcasted_iota(jnp.int32, lst.shape, 1) < counts[...]
    mine = live & (lst // BLK == me)
    within = lst % BLK
    lo = jnp.min(jnp.where(mine, within, 1000), 1, keepdims=True)
    hi = jnp.max(jnp.where(mine, within, -1), 1, keepdims=True)
    hi = jnp.where(hi == lo, 1000, hi)
    lo = jnp.where(lo < 0, 1000, lo)
    hi = jnp.where(hi < 0, 1000, hi)
    readers = lst.shape[0]
    lo_b = jnp.broadcast_to(lo.astype(F32), (readers, 256)).astype(BF)
    hi_b = jnp.broadcast_to(hi.astype(F32), (readers, 256)).astype(BF)

    row = lists[pl.ds(me, 1), :]
    n_live = counts[pl.ds(me, 1), :]
    row_live = lax.broadcasted_iota(jnp.int32, row.shape, 1) < n_live
    owner = lax.broadcasted_iota(jnp.int32, lst.shape, 0)
    n_of = jnp.sum(jnp.where((row // BLK == owner) & row_live, 1, 0), 1, keepdims=True)
    for x1 in range(NX):
        key = lax.broadcasted_iota(jnp.int32, (readers, 256), 1)
        own_of = lax.broadcasted_iota(jnp.int32, (readers, 256), 0)
        cnt = jnp.sum(jnp.where(own_of == x1 * NZ + key // 32, n_of, 0), 0, keepdims=True)
        part = (lax.broadcasted_iota(jnp.int32, (1, 256), 1) // BLK) % 2
        seen[x1] = jnp.broadcast_to(jnp.where(cnt > part, 1.0, 0.0), (8, 256))

    def pack(x2):
        r = lax.broadcasted_iota(jnp.int32, (256, readers), 0) // 32 + x2 * NZ
        pick = (r == lax.broadcasted_iota(jnp.int32, (256, readers), 1)).astype(F32).astype(BF)
        first = jnp.dot(pick, lo_b, preferred_element_type=F32)
        second = jnp.dot(pick, hi_b, preferred_element_type=F32)
        rows = lax.broadcasted_iota(jnp.int32, (256, 256), 0)
        cols = lax.broadcasted_iota(jnp.int32, (256, 256), 1)
        blk = jnp.where((rows // BLK) % 2 == 0, first, second)
        want = blk * BLK + (rows % BLK).astype(F32)
        hot[...] = jnp.where(want == cols.astype(F32), 1.0, 0.0).astype(BF)
        sk[x2] = jnp.dot(hot[...], kc[...], preferred_element_type=F32).astype(BF).reshape(NZ, 32, kc.shape[1])
        sv[x2] = jnp.dot(hot[...], vc[...], preferred_element_type=F32).astype(BF).reshape(NZ, 32, kc.shape[1])

    loop(x, NX, pack)
    wz[z, x] = wt[x]
    pl.semaphore_wait(barrier, NX - 1 + NZ - 1 + 1)

    for d in (1, 3, 2):
        x2 = (x + d) % NX
        remote(wt.at[x2], wz.at[z, x], w1s.at[x2], w1r.at[x], slot=at(x2, z)).start()
    for d in RING + (0,):
        z2 = (z + d) % NZ
        if d:
            @pl.when(z2 > z)
            def _():
                remote(sk.at[x, z2], rk.at[x, z], os.at[0, z2], orr.at[0, z], slot=at(x, z2)).start()
                remote(sv.at[x, z2], rv.at[x, z], os.at[1, z2], orr.at[1, z], slot=at(x, z2)).start()

        def out(x2):
            if d:
                remote(sk.at[x2, z2], kb.at[x, z2], k1s.at[x2, z2], k1r.at[x, z2], slot=at(x2, z)).start()
                remote(sv.at[x2, z2], vb.at[x2, z], v1s.at[x2, z2], v1r.at[x2, z], slot=at(x, z2)).start()
            else:
                remote(sk.at[x2, z], rk.at[x, z], k2s.at[x2, z], k2r.at[x, z], slot=at(x2, z)).start()
                remote(sv.at[x2, z], rv.at[x, z], v2s.at[x2, z], v2r.at[x, z], slot=at(x2, z)).start()

        loop(x + 1, NX, out)

    def blank(z1):
        rk[x, z1] = jnp.zeros(rk.shape[2:], BF)
        rv[x, z1] = jnp.zeros(rv.shape[2:], BF)

    loop(z, NZ, blank)

    for h in range(heads):
        cols = slice(h * HD, (h + 1) * HD)
        s = lax.dot_general(q[:, cols], kn[:, cols], NT, preferred_element_type=F32)
        top = jnp.max(s, 1, keepdims=True)
        p = jnp.exp2((s - top) * c2)
        mx[h] = jnp.broadcast_to(top, (256, HD))
        tot[h] = jnp.broadcast_to(jnp.sum(p, 1, keepdims=True), (256, HD))
        acc[:, cols] = jnp.dot(p.astype(BF), vn[:, cols], preferred_element_type=F32)

    def ring_step(k):
        zp, zm = (z + 1) % NZ, (z + NZ - 1) % NZ
        a, b = (z + NZ - k + 1) % NZ, (z + k - 1) % NZ
        if k > 1:
            remote(wz.at[a], wz.at[a], wps.at[k - 2], wpr.at[k - 2], slot=at(x, zp)).wait_recv()
            remote(wz.at[b], wz.at[b], wms.at[k - 2], wmr.at[k - 2], slot=at(x, zm)).wait_recv()
        if k < 4:
            remote(wz.at[a], wz.at[a], wps.at[k - 1], wpr.at[k - 1], slot=at(x, zp)).start()
            remote(wz.at[b], wz.at[b], wms.at[k - 1], wmr.at[k - 1], slot=at(x, zm)).start()
        else:
            remote(wz.at[a, pl.ds(0, 2)], wz.at[a, pl.ds(0, 2)], wps.at[3], wpr.at[3], slot=at(x, zp)).start()
            remote(wz.at[b, pl.ds(2, 2)], wz.at[b, pl.ds(2, 2)], wms.at[3], wmr.at[3], slot=at(x, zm)).start()

    for d in (1, 3, 2):
        x1 = (x + d) % NX
        remote(wt.at[x], wz.at[z, x1], w1s.at[x1], w1r.at[x1], slot=at(x1, z)).wait_recv()
    ring_step(1)

    for i, d in enumerate(RING):
        z2 = (z + d) % NZ

        def fwd_k(x1):
            remote(kb.at[x1, z2], kb.at[x1, z2], k1s.at[x, z2], k1r.at[x1, z2], slot=me).wait_recv()
            remote(kb.at[x1, z2], rk.at[x1, z], k2s.at[x1, z2], k2r.at[x1, z], slot=at(x, z2)).start()

        def fwd_v(x2):
            remote(vb.at[x2, z2], vb.at[x2, z2], v1s.at[x, z2], v1r.at[x2, z2], slot=me).wait_recv()
            remote(vb.at[x2, z2], rv.at[x, z2], v2s.at[x2, z2], v2r.at[x, z2], slot=at(x2, z)).start()

        loop(x + 1, NX, fwd_v)
        loop(0, x, fwd_k)
        if i == 3:
            ring_step(2)
    ring_step(3)

    def chunk(x1):
        ok = seen[x1][0:1, :] > 0.5
        for h in range(heads):
            cols = slice(h * HD, (h + 1) * HD)
            keys = rk[x1, :, :, cols].reshape(256, HD)
            vals = rv[x1, :, :, cols].reshape(256, HD)
            s = lax.dot_general(q[:, cols], keys, NT, preferred_element_type=F32)
            s = jnp.where(ok, s, NEG)
            old = mx[h][:, :1]
            top = jnp.maximum(old, jnp.max(s, 1, keepdims=True))
            fade = jnp.exp2((old - top) * c2)
            p = jnp.exp2((s - top) * c2)
            mx[h] = jnp.broadcast_to(top, (256, HD))
            tot[h] = tot[h] * fade + jnp.sum(p, 1, keepdims=True)
            acc[:, cols] = acc[:, cols] * fade + jnp.dot(p.astype(BF), vals, preferred_element_type=F32)

    def own_row(z1):
        remote(sk.at[x, z1], rk.at[x, z1], os.at[0, z1], orr.at[0, z1], slot=me).wait_recv()
        remote(sv.at[x, z1], rv.at[x, z1], os.at[1, z1], orr.at[1, z1], slot=me).wait_recv()

    loop(0, z, own_row)
    chunk(x)
    ring_step(4)

    def earlier(i):
        x1 = x - 1 - i
        for z1 in range(NZ):
            remote(sk.at[x1, z1], rk.at[x1, z1], k2s.at[x1, z1], k2r.at[x1, z1], slot=me).wait_recv()
            remote(sv.at[x1, z1], rv.at[x1, z1], v2s.at[x1, z1], v2r.at[x1, z1], slot=me).wait_recv()
        chunk(x1)

    loop(0, x, earlier)
    for h in range(heads):
        cols = slice(h * HD, (h + 1) * HD)
        attn[:, cols] = (acc[:, cols] / tot[h]).astype(BF)

    far = (z + 4) % NZ
    remote(wz.at[far, pl.ds(0, 2)], wz.at[far, pl.ds(0, 2)], wps.at[3], wpr.at[3], slot=me).wait_recv()
    remote(wz.at[far, pl.ds(2, 2)], wz.at[far, pl.ds(2, 2)], wms.at[3], wmr.at[3], slot=me).wait_recv()
    other = (1 - core) * 4
    swap = remote(wz.at[pl.ds(other, 4)], wall.at[core], wcs, wcr, tp=sib)
    swap.start()
    wall[core] = wz[pl.ds(core * 4, 4)]

    for d in (1, 3, 2):
        x2 = (x + d) % NX
        remote(wt.at[x2], wz.at[z, x], w1s.at[x2], w1r.at[x], slot=at(x2, z)).wait_send()
    for k in range(3):
        remote(wz.at[z], wz.at[z], wps.at[k], wpr.at[k], slot=me).wait_send()
        remote(wz.at[z], wz.at[z], wms.at[k], wmr.at[k], slot=me).wait_send()
    remote(wz.at[z, pl.ds(0, 2)], wz.at[z, pl.ds(0, 2)], wps.at[3], wpr.at[3], slot=me).wait_send()
    remote(wz.at[z, pl.ds(2, 2)], wz.at[z, pl.ds(2, 2)], wms.at[3], wmr.at[3], slot=me).wait_send()
    for d in RING + (0,):
        z2 = (z + d) % NZ
        if d:
            @pl.when(z2 > z)
            def _():
                remote(sk.at[x, z2], rk.at[x, z], os.at[0, z2], orr.at[0, z], slot=me).wait_send()
                remote(sv.at[x, z2], rv.at[x, z], os.at[1, z2], orr.at[1, z], slot=me).wait_send()

        def sent(x2):
            if d:
                remote(sk.at[x2, z2], kb.at[x, z2], k1s.at[x2, z2], k1r.at[x, z2], slot=me).wait_send()
                remote(sv.at[x2, z2], vb.at[x2, z], v1s.at[x2, z2], v1r.at[x2, z], slot=me).wait_send()
                remote(vb.at[x2, z2], rv.at[x, z2], v2s.at[x2, z2], v2r.at[x, z2], slot=me).wait_send()
            else:
                remote(sk.at[x2, z], rk.at[x, z], k2s.at[x2, z], k2r.at[x, z], slot=me).wait_send()
                remote(sv.at[x2, z], rv.at[x, z], v2s.at[x2, z], v2r.at[x, z], slot=me).wait_send()

        def passed(x1):
            remote(kb.at[x1, z2], rk.at[x1, z], k2s.at[x1, z2], k2r.at[x1, z], slot=me).wait_send()

        loop(x + 1, NX, sent)
        if d:
            loop(0, x, passed)
    swap.wait()


def projection_kernel(
    attn, w, resid,
    out,
    a, part, got, red, fin, flat,
    cs, cr, a1s, a1r, a2s, a2r, ys, yr, xs_, xr,
):
    me = lax.axis_index("slot")
    tp = lax.axis_index("tp")
    x, z, y, core = me // NZ, me % NZ, tp // 2, tp % 2
    sib = tp + 1 - 2 * core

    def at(ax):
        return ax * NZ + z

    left, right, across = (x + 3) % NX, (x + 1) % NX, (x + 2) % NX
    barrier = pltpu.get_barrier_semaphore()
    for d in range(1, NX):
        pl.semaphore_signal(barrier, inc=1, device_id={"slot": at((x + d) % NX)}, device_id_type=MESH)
        pl.semaphore_signal(barrier, inc=1, device_id={"tp": ((y + d) % NY) * 2 + core}, device_id_type=MESH)
    pl.semaphore_signal(barrier, inc=1, device_id={"tp": sib}, device_id_type=MESH)
    a[core, x] = attn[...]
    pl.semaphore_wait(barrier, NX - 1 + NY - 1 + 1)

    def to_sib(g):
        return remote(a.at[core, g], a.at[core, g], cs.at[g], cr.at[g], tp=sib)

    def from_sib(g):
        remote(a.at[1 - core, g], a.at[1 - core, g], cs.at[g], cr.at[g], tp=sib).wait_recv()

    to_sib(x).start()
    to_right = remote(a.at[core, x], a.at[core, x], a1s.at[0], a1r.at[0], slot=at(right))
    to_left = remote(a.at[core, x], a.at[core, x], a1s.at[1], a1r.at[1], slot=at(left))
    to_right.start()
    to_left.start()

    def share(g, d, peer):
        return remote(part.at[g, peer], got.at[g, y], ys.at[g, d - 1], yr.at[g, d - 1], tp=peer * 2 + core)

    def project(g):
        from_sib(g)
        for zs in range(4):
            o = lax.dot_general(w[0, zs].reshape(192, 768), a[0, g], NT, preferred_element_type=F32)
            o += lax.dot_general(w[1, zs].reshape(192, 768), a[1, g], NT, preferred_element_type=F32)
            for p in range(NY):
                part[g, p, zs * 48 : (zs + 1) * 48, :] = o[p * 48 : (p + 1) * 48].astype(BF)
        for d in (1, 3, 2):
            share(g, d, (y + d) % NY).start()

    def reduce(g):
        s = part[g, y].astype(F32)
        for d in (1, 3, 2):
            src = (y + NY - d) % NY
            remote(part.at[g, y], got.at[g, src], ys.at[g, d - 1], yr.at[g, d - 1], slot=me).wait_recv()
            s += got[g, src].astype(F32)
        return s.astype(BF)

    def home(d):
        g = (x + d) % NX
        return remote(red.at[g], fin.at[x], xs_.at[d - 1], xr.at[d - 1], slot=at(g))

    project(x)
    remote(a.at[core, left], a.at[core, left], a1s.at[0], a1r.at[0], slot=me).wait_recv()
    half_r = remote(a.at[core, left, pl.ds(0, 128)], a.at[core, left, pl.ds(0, 128)], a2s.at[0], a2r.at[0], slot=at(right))
    half_r.start()
    to_sib(left).start()
    remote(a.at[core, right], a.at[core, right], a1s.at[1], a1r.at[1], slot=me).wait_recv()
    half_l = remote(a.at[core, right, pl.ds(128, 128)], a.at[core, right, pl.ds(128, 128)], a2s.at[1], a2r.at[1], slot=at(left))
    half_l.start()
    to_sib(right).start()
    project(left)
    project(right)
    fin[x] = reduce(x)
    remote(a.at[core, across, pl.ds(0, 128)], a.at[core, across, pl.ds(0, 128)], a2s.at[0], a2r.at[0], slot=me).wait_recv()
    remote(a.at[core, across, pl.ds(128, 128)], a.at[core, across, pl.ds(128, 128)], a2s.at[1], a2r.at[1], slot=me).wait_recv()
    to_sib(across).start()
    project(across)
    for d in (3, 1, 2):
        g = (x + d) % NX
        red[g] = reduce(g)
        home(d).start()
    for d in (3, 1, 2):
        src = (x + NX - d) % NX
        remote(red.at[x], fin.at[src], xs_.at[d - 1], xr.at[d - 1], slot=me).wait_recv()
    for src in range(NX):
        for zs in range(4):
            flat[zs * 192 + src * 48 : zs * 192 + (src + 1) * 48, :] = fin[src, zs * 48 : (zs + 1) * 48, :]
    rows = lax.broadcasted_iota(jnp.int32, (256, 256), 0)
    cols = lax.broadcasted_iota(jnp.int32, (256, 256), 1)
    eye = jnp.where(rows == cols, 1.0, 0.0).astype(BF)
    summed = lax.dot_general(eye, flat[...], NT, preferred_element_type=F32)
    out[...] = (resid[...].astype(F32) + summed).astype(BF)

    for g in range(NX):
        to_sib(g).wait_send()
        for d in range(1, NY):
            share(g, d, (y + d) % NY).wait_send()
    to_right.wait_send()
    to_left.wait_send()
    half_r.wait_send()
    half_l.wait_send()
    for d in range(1, NX):
        home(d).wait_send()


def per_device(queries, k_new, v_new, k_clean, v_clean, lists, counts, resid, w_out):
    width = queries.shape[1]
    wt = w_out.T.reshape(NX, 48, width)
    vm = pl.BlockSpec(memory_space=VM)
    attn, wall = pl.pallas_call(
        attention_kernel,
        out_shape=(
            jax.ShapeDtypeStruct((256, width), BF),
            jax.ShapeDtypeStruct((2, 4, NX, 48, width), BF),
        ),
        in_specs=[vm] * 8,
        out_specs=(vm, vm),
        scratch_shapes=[
            VM((NX, NZ, 32, width), BF), VM((NX, NZ, 32, width), BF),
            VM((NX, NZ, 32, width), BF), VM((NX, NZ, 32, width), BF),
            VM((NX, NZ, 32, width), BF), VM((NX, NZ, 32, width), BF),
            VM((NZ, NX, 48, width), BF), VM((256, 256), BF), VM((NX, 8, 256), F32),
            VM((width // HD, 256, HD), F32), VM((width // HD, 256, HD), F32), VM((256, width), F32),
            DMA((NX, NZ)), DMA((NX, NZ)), DMA((NX, NZ)), DMA((NX, NZ)),
            DMA((NX, NZ)), DMA((NX, NZ)), DMA((NX, NZ)), DMA((NX, NZ)),
            DMA((2, NZ)), DMA((2, NZ)), DMA((NX,)), DMA((NX,)),
            DMA((4,)), DMA((4,)), DMA((4,)), DMA((4,)), DMA, DMA,
        ],
        compiler_params=pltpu.CompilerParams(
            collective_id=0, has_side_effects=True, vmem_limit_bytes=56 << 20
        ),
        name="attention",
    )(queries, k_new, v_new, k_clean, v_clean, wt, lists, counts.reshape(-1, 1))
    return pl.pallas_call(
        projection_kernel,
        out_shape=jax.ShapeDtypeStruct((256, width), BF),
        in_specs=[vm] * 3,
        out_specs=vm,
        scratch_shapes=[
            VM((2, NX, 256, width), BF), VM((NX, NY, 192, 256), BF), VM((NX, NY, 192, 256), BF),
            VM((NX, 192, 256), BF), VM((NX, 192, 256), BF), VM((width, 256), BF),
            DMA((NX,)), DMA((NX,)), DMA((2,)), DMA((2,)), DMA((2,)), DMA((2,)),
            DMA((NX, 3)), DMA((NX, 3)), DMA((3,)), DMA((3,)),
        ],
        compiler_params=pltpu.CompilerParams(
            collective_id=1, has_side_effects=True, vmem_limit_bytes=56 << 20
        ),
        name="projection",
    )(attn, wall, resid)


def solution(mesh):
    in_specs = (
        P("slot", "tp"),
        P("slot", "tp"),
        P("slot", "tp"),
        P("slot", "tp"),
        P("slot", "tp"),
        P(),
        P(),
        P("slot", "tp"),
        P("tp", "slot"),
    )
    out_specs = P("slot", "tp")
    return jax.shard_map(
        per_device, mesh=mesh, in_specs=in_specs, out_specs=out_specs, check_vma=False
    )
```

```python
import math

import jax
import jax.numpy as jnp
from jax import lax
from jax.experimental import pallas as pl
from jax.experimental.pallas import tpu as pltpu
from jax.sharding import PartitionSpec as P

HD = 128
BLK = 16
NX, NZ, NY = 4, 8, 4
RING = (1, 7, 2, 6, 3, 5, 4)
MESH = pl.DeviceIdType.MESH
BF = jnp.bfloat16
F32 = jnp.float32
NEG = -1e30
NT = (((1,), (1,)), ((), ()))
VM = pltpu.VMEM
DMA = pltpu.SemaphoreType.DMA


def remote(src, dst, ssem, rsem, **where):
    return pltpu.make_async_remote_copy(
        src_ref=src, dst_ref=dst, send_sem=ssem, recv_sem=rsem, device_id=where, device_id_type=MESH
    )


def loop(lo, hi, body):
    def step(i, c):
        body(i)
        return c

    lax.fori_loop(lo, hi, step, 0)


def layer_kernel(
    q, kn, vn, kc, vc, wt, lists, counts, resid,
    out,
    sk, sv, kb, vb, rk, rv, wz, ws, seen, mx, tot, acc, tab, tabs,
    a, part, got, red, fin, flat,
    ts, k1s, k1r, k2s, k2r, v1s, v1r, v2s, v2r, os, orr, w1s, w1r, wps, wpr, wms, wmr, wcs, wcr,
    cs, cr, a1s, a1r, a2s, a2r, ys, yr, hs, hr,
):
    me = lax.axis_index("slot")
    tp = lax.axis_index("tp")
    x, z, y, core = me // NZ, me % NZ, tp // 2, tp % 2
    sib = tp + 1 - 2 * core
    left, right, across = (x + 3) % NX, (x + 1) % NX, (x + 2) % NX
    heads = q.shape[1] // HD
    c2 = math.log2(math.e) / math.sqrt(HD)

    def at(ax, az):
        return ax * NZ + az

    def put(src, dst, ssem, rsem, **where):
        remote(src, dst, ssem, rsem, **where).start()

    def take(dst, rsem):
        remote(dst, dst, rsem, rsem, slot=me).wait_recv()

    def sent(src, ssem):
        remote(src, src, ssem, ssem, slot=me).wait_send()

    barrier = pltpu.get_barrier_semaphore()
    for d in range(1, NX):
        pl.semaphore_signal(barrier, inc=1, device_id={"slot": at((x + d) % NX, z)}, device_id_type=MESH)
    for d in range(1, NZ):
        pl.semaphore_signal(barrier, inc=1, device_id={"slot": at(x, (z + d) % NZ)}, device_id_type=MESH)
    for d in range(1, NY):
        pl.semaphore_signal(barrier, inc=1, device_id={"tp": ((y + d) % NY) * 2 + core}, device_id_type=MESH)
    pl.semaphore_signal(barrier, inc=1, device_id={"tp": sib}, device_id_type=MESH)

    lst = lists[...]
    readers = lst.shape[0]
    sub = lax.broadcasted_iota(jnp.int32, (readers, 128), 0)
    lane = lax.broadcasted_iota(jnp.int32, (readers, 128), 1)
    live_n = jnp.sum(jnp.where(sub[:, :readers] == lane[:, :readers], counts[...], 0), 1, keepdims=True)
    live = lax.broadcasted_iota(jnp.int32, lst.shape, 1) < live_n
    mine = live & (lst // BLK == me)
    within = lst % BLK
    lo = jnp.min(jnp.where(mine, within, BLK), 1, keepdims=True)
    hi = jnp.max(jnp.where(mine, within, 0), 1, keepdims=True)
    lo = jnp.where(lo < BLK, lo, 0)
    tab[0:1, :] = jnp.sum(jnp.where(sub == lane, lo, 0), 0, keepdims=True)
    tab[1:2, :] = jnp.sum(jnp.where(sub == lane, hi, 0), 0, keepdims=True)
    to_scalar = pltpu.make_async_copy(tab, tabs, ts)
    to_scalar.start()

    row = lists[pl.ds(me, 1), :]
    n_live = jnp.sum(jnp.where(lax.broadcasted_iota(jnp.int32, counts.shape, 1) == me, counts[...], 0), 1, keepdims=True)
    row_live = lax.broadcasted_iota(jnp.int32, row.shape, 1) < n_live
    owner = lax.broadcasted_iota(jnp.int32, lst.shape, 0)
    n_of = jnp.sum(jnp.where((row // BLK == owner) & row_live, 1, 0), 1, keepdims=True)
    for x1 in range(NX):
        key = lax.broadcasted_iota(jnp.int32, (readers, 256), 1)
        own_of = lax.broadcasted_iota(jnp.int32, (readers, 256), 0)
        cnt = jnp.sum(jnp.where(own_of == x1 * NZ + key // 32, n_of, 0), 0, keepdims=True)
        odd = (lax.broadcasted_iota(jnp.int32, (1, 256), 1) // BLK) % 2
        seen[x1] = jnp.broadcast_to(jnp.where(cnt > odd, 1.0, 0.0), (8, 256))
    to_scalar.wait()

    def pack(x2):
        for z2 in range(NZ):
            r = at(x2, z2)
            for half in range(2):
                blk = tabs[half, r]
                sk[x2, z2, half * BLK : (half + 1) * BLK, :] = kc[blk]
                sv[x2, z2, half * BLK : (half + 1) * BLK, :] = vc[blk]

    pack(x)
    pl.semaphore_wait(barrier, NX - 1 + NZ - 1 + NY - 1 + 1)

    for d in RING:
        z2 = (z + d) % NZ

        @pl.when(z2 > z)
        def _():
            put(sk.at[x, z2], rk.at[x, z], os.at[0, z2], orr.at[0, z], slot=at(x, z2))
            put(sv.at[x, z2], rv.at[x, z], os.at[1, z2], orr.at[1, z], slot=at(x, z2))

    def give(x2):
        pack(x2)
        for d in RING:
            z2 = (z + d) % NZ
            put(sv.at[x2, z2], vb.at[x2, z], v1s.at[x2, z2], v1r.at[x2, z], slot=at(x, z2))
            put(sk.at[x2, z2], kb.at[x, z2], k1s.at[x2, z2], k1r.at[x, z2], slot=at(x2, z))
        put(sk.at[x2, z], rk.at[x, z], k2s.at[x2, z], k2r.at[x, z], slot=at(x2, z))
        put(sv.at[x2, z], rv.at[x, z], v2s.at[x2, z], v2r.at[x, z], slot=at(x2, z))

    loop(x + 1, NX, give)
    for d in (1, 3, 2):
        x2 = (x + d) % NX
        put(wt.at[x2], wz.at[z, x], w1s.at[x2], w1r.at[x], slot=at(x2, z))
    wz[z, x] = wt[x]

    def blank(z1):
        rk[x, z1] = jnp.zeros(rk.shape[2:], BF)
        rv[x, z1] = jnp.zeros(rv.shape[2:], BF)

    loop(z, NZ, blank)

    for h in range(heads):
        cols = slice(h * HD, (h + 1) * HD)
        s = lax.dot_general(q[:, cols], kn[:, cols], NT, preferred_element_type=F32)
        top = jnp.max(s, 1, keepdims=True)
        p = jnp.exp2((s - top) * c2)
        mx[h] = jnp.broadcast_to(top, (256, HD))
        tot[h] = jnp.broadcast_to(jnp.sum(p, 1, keepdims=True), (256, HD))
        acc[:, cols] = jnp.dot(p.astype(BF), vn[:, cols], preferred_element_type=F32)

    def chunk(x1):
        ok = seen[x1][0:1, :] > 0.5
        for h in range(heads):
            cols = slice(h * HD, (h + 1) * HD)
            keys = rk[x1, :, :, cols].reshape(256, HD)
            vals = rv[x1, :, :, cols].reshape(256, HD)
            s = lax.dot_general(q[:, cols], keys, NT, preferred_element_type=F32)
            s = jnp.where(ok, s, NEG)
            old = mx[h][:, :1]
            top = jnp.maximum(old, jnp.max(s, 1, keepdims=True))
            fade = jnp.exp2((old - top) * c2)
            p = jnp.exp2((s - top) * c2)
            mx[h] = jnp.broadcast_to(top, (256, HD))
            tot[h] = tot[h] * fade + jnp.sum(p, 1, keepdims=True)
            acc[:, cols] = acc[:, cols] * fade + jnp.dot(p.astype(BF), vals, preferred_element_type=F32)

    def w_pass(zs, sem):
        @pl.when(zs // 4 != core)
        def _():
            put(wz.at[zs], ws.at[zs % 4], wcs.at[zs % 4], wcr.at[zs % 4], tp=sib)

    def ring_step(k):
        zp, zm = (z + 1) % NZ, (z + NZ - 1) % NZ
        up, dn = (z + NZ - k + 1) % NZ, (z + k - 1) % NZ
        if k > 1:
            take(wz.at[up], wpr.at[k - 2])
            take(wz.at[dn], wmr.at[k - 2])
        if k < 4:
            put(wz.at[up], wz.at[up], wps.at[k - 1], wpr.at[k - 1], slot=at(x, zp))
            put(wz.at[dn], wz.at[dn], wms.at[k - 1], wmr.at[k - 1], slot=at(x, zm))
        else:
            put(wz.at[up, pl.ds(0, 2)], wz.at[up, pl.ds(0, 2)], wps.at[3], wpr.at[3], slot=at(x, zp))
            put(wz.at[dn, pl.ds(2, 2)], wz.at[dn, pl.ds(2, 2)], wms.at[3], wmr.at[3], slot=at(x, zm))
        w_pass(up, 0)
        if k > 1:
            w_pass(dn, 0)

    for d in (1, 3, 2):
        x1 = (x + d) % NX
        take(wz.at[z, x1], w1r.at[x1])
    def fwd_k(i):
        x1 = x - 1 - i
        for d in RING:
            z2 = (z + d) % NZ
            take(kb.at[x1, z2], k1r.at[x1, z2])
            put(kb.at[x1, z2], rk.at[x1, z], k2s.at[x1, z2], k2r.at[x1, z], slot=at(x, z2))

    loop(0, x, fwd_k)
    ring_step(1)

    def own_row(z1):
        take(rk.at[x, z1], orr.at[0, z1])
        take(rv.at[x, z1], orr.at[1, z1])

    loop(0, z, own_row)
    chunk(x)

    for i, d in enumerate(RING):
        z2 = (z + d) % NZ

        def fwd_v(x2):
            take(vb.at[x2, z2], v1r.at[x2, z2])
            put(vb.at[x2, z2], rv.at[x, z2], v2s.at[x2, z2], v2r.at[x, z2], slot=at(x2, z))

        loop(x + 1, NX, fwd_v)
    ring_step(2)

    def earlier(i):
        x1 = x - 1 - i
        for z1 in range(NZ):
            take(rk.at[x1, z1], k2r.at[x1, z1])
            take(rv.at[x1, z1], v2r.at[x1, z1])
        chunk(x1)

    loop(0, x, earlier)
    for h in range(heads):
        cols = slice(h * HD, (h + 1) * HD)
        a[core, x, :, cols] = (acc[:, cols] / tot[h]).astype(BF)

    def to_sib(g):
        return remote(a.at[core, g], a.at[core, g], cs.at[g], cr.at[g], tp=sib)

    to_sib(x).start()
    put(a.at[core, x], a.at[core, x], a1s.at[0], a1r.at[0], slot=at(right, z))
    put(a.at[core, x], a.at[core, x], a1s.at[1], a1r.at[1], slot=at(left, z))

    def tile(g, zl):
        zs = core * 4 + zl
        o = lax.dot_general(wz[zs].reshape(192, 768), a[core, g], NT, preferred_element_type=F32)
        o += lax.dot_general(ws[zl].reshape(192, 768), a[1 - core, g], NT, preferred_element_type=F32)
        for p in range(NY):
            part[g, p, zl] = o[p * 48 : (p + 1) * 48].astype(BF)
        for d in (1, 3, 2):
            p = (y + d) % NY
            put(part.at[g, p, zl], got.at[g, y, zl], ys.at[g, zl, d - 1], yr.at[g, zl, d - 1], tp=p * 2 + core)

    def tiles(j0, j1, k0, k1):
        def one(j):
            g = (x + (j % 2) * 3 + (j // 2) * (1 - 2 * (j % 2)) + NX) % NX

            def two(k):
                d = (k % 2) * ((k + 1) // 2) + (1 - k % 2) * ((NZ - k // 2) % NZ)
                zs = (z + d) % NZ

                @pl.when(zs // 4 == core)
                def _():
                    if j0 == 0:
                        take(ws.at[zs % 4], wcr.at[zs % 4])
                    tile(g, zs % 4)

            loop(k0, k1, two)

        loop(j0, j1, one)

    take(a.at[1 - core, x], cr.at[x])
    tiles(0, 1, 0, 3)
    ring_step(3)
    tiles(0, 1, 3, 5)
    take(a.at[core, left], a1r.at[0])
    put(a.at[core, left, pl.ds(0, 128)], a.at[core, left, pl.ds(0, 128)], a2s.at[0], a2r.at[0], slot=at(right, z))
    to_sib(left).start()
    take(a.at[core, right], a1r.at[1])
    put(a.at[core, right, pl.ds(128, 128)], a.at[core, right, pl.ds(128, 128)], a2s.at[1], a2r.at[1], slot=at(left, z))
    to_sib(right).start()
    take(a.at[1 - core, left], cr.at[left])
    take(a.at[1 - core, right], cr.at[right])
    tiles(1, 3, 0, 5)
    ring_step(4)
    tiles(0, 1, 5, 7)
    tiles(1, 3, 5, 7)
    take(a.at[core, across, pl.ds(0, 128)], a2r.at[0])
    take(a.at[core, across, pl.ds(128, 128)], a2r.at[1])
    to_sib(across).start()
    take(a.at[1 - core, across], cr.at[across])
    tiles(3, 4, 0, 7)
    far = (z + 4) % NZ
    take(wz.at[far, pl.ds(0, 2)], wpr.at[3])
    take(wz.at[far, pl.ds(2, 2)], wmr.at[3])
    w_pass(far, 0)
    tiles(0, 1, 7, 8)
    tiles(1, 4, 7, 8)

    def reduce(g):
        s = part[g, y].astype(F32)
        for d in (1, 3, 2):
            src = (y + NY - d) % NY
            for zl in range(4):
                take(got.at[g, src, zl], yr.at[g, zl, d - 1])
            s += got[g, src].astype(F32)
        return s.astype(BF)

    for d in (3, 1, 2):
        g = (x + d) % NX
        red[g] = reduce(g)
        put(red.at[g], fin.at[x], hs.at[d - 1], hr.at[d - 1], slot=at(g, z))
    fin[x] = reduce(x)
    for d in (3, 1, 2):
        take(fin.at[(x + NX - d) % NX], hr.at[d - 1])
    for src in range(NX):
        for zs in range(4):
            flat[zs * 192 + src * 48 : zs * 192 + (src + 1) * 48, :] = fin[src, zs]
    rows = lax.broadcasted_iota(jnp.int32, (256, 256), 0)
    cols = lax.broadcasted_iota(jnp.int32, (256, 256), 1)
    eye = jnp.where(rows == cols, 1.0, 0.0).astype(BF)
    summed = lax.dot_general(eye, flat[...], NT, preferred_element_type=F32)
    out[...] = (resid[...].astype(F32) + summed).astype(BF)

    for d in (1, 3, 2):
        x2 = (x + d) % NX
        sent(wt.at[x2], w1s.at[x2])
        sent(red.at[x2], hs.at[d - 1])
    for k in range(3):
        sent(wz.at[z], wps.at[k])
        sent(wz.at[z], wms.at[k])
    sent(wz.at[z, pl.ds(0, 2)], wps.at[3])
    sent(wz.at[z, pl.ds(2, 2)], wms.at[3])
    for zl in range(4):
        sent(wz.at[z], wcs.at[zl])
    for g in range(NX):
        sent(a.at[core, g], cs.at[g])
    for i in range(2):
        sent(a.at[core, x], a1s.at[i])
        sent(a.at[core, x, pl.ds(0, 128)], a2s.at[i])

    def tile_sent(g):
        for zl in range(4):
            for d in range(3):
                sent(part.at[g, 0, zl], ys.at[g, zl, d])

    loop(0, NX, tile_sent)
    for d in RING:
        z2 = (z + d) % NZ

        @pl.when(z2 > z)
        def _():
            sent(sk.at[x, z2], os.at[0, z2])
            sent(sv.at[x, z2], os.at[1, z2])

        def given(x2):
            sent(sk.at[x2, z2], k1s.at[x2, z2])
            sent(sv.at[x2, z2], v1s.at[x2, z2])
            sent(vb.at[x2, z2], v2s.at[x2, z2])

        def passed(x1):
            sent(kb.at[x1, z2], k2s.at[x1, z2])

        loop(x + 1, NX, given)
        loop(0, x, passed)

    def straight(x2):
        sent(sk.at[x2, z], k2s.at[x2, z])
        sent(sv.at[x2, z], v2s.at[x2, z])

    loop(x + 1, NX, straight)


def per_device(queries, k_new, v_new, k_clean, v_clean, lists, counts, resid, w_out):
    width = queries.shape[1]
    wt = w_out.T.reshape(NX, 48, width)
    blocks = (-1, BLK, width)
    vm = pl.BlockSpec(memory_space=VM)
    heads = width // HD
    return pl.pallas_call(
        layer_kernel,
        out_shape=jax.ShapeDtypeStruct((256, width), BF),
        in_specs=[vm] * 9,
        out_specs=vm,
        scratch_shapes=[
            VM((NX, NZ, 32, width), BF), VM((NX, NZ, 32, width), BF),
            VM((NX, NZ, 32, width), BF), VM((NX, NZ, 32, width), BF),
            VM((NX, NZ, 32, width), BF), VM((NX, NZ, 32, width), BF),
            VM((NZ, NX, 48, width), BF), VM((4, NX, 48, width), BF), VM((NX, 8, 256), F32),
            VM((heads, 256, HD), F32), VM((heads, 256, HD), F32), VM((256, width), F32),
            VM((8, 128), jnp.int32), pltpu.SMEM((8, 128), jnp.int32),
            VM((2, NX, 256, width), BF), VM((NX, NY, 4, 48, 256), BF), VM((NX, NY, 4, 48, 256), BF),
            VM((NX, 4, 48, 256), BF), VM((NX, 4, 48, 256), BF), VM((width, 256), BF),
            DMA, DMA((NX, NZ)), DMA((NX, NZ)), DMA((NX, NZ)), DMA((NX, NZ)),
            DMA((NX, NZ)), DMA((NX, NZ)), DMA((NX, NZ)), DMA((NX, NZ)),
            DMA((2, NZ)), DMA((2, NZ)), DMA((NX,)), DMA((NX,)),
            DMA((4,)), DMA((4,)), DMA((4,)), DMA((4,)), DMA((4,)), DMA((4,)),
            DMA((NX,)), DMA((NX,)), DMA((2,)), DMA((2,)), DMA((2,)), DMA((2,)),
            DMA((NX, 4, 3)), DMA((NX, 4, 3)), DMA((3,)), DMA((3,)),
        ],
        compiler_params=pltpu.CompilerParams(
            collective_id=0, has_side_effects=True, vmem_limit_bytes=56 << 20
        ),
        name="layer",
    )(
        queries, k_new, v_new, k_clean.reshape(blocks), v_clean.reshape(blocks), wt,
        lists, counts.reshape(1, -1), resid,
    )


def solution(mesh):
    in_specs = (
        P("slot", "tp"),
        P("slot", "tp"),
        P("slot", "tp"),
        P("slot", "tp"),
        P("slot", "tp"),
        P(),
        P(),
        P("slot", "tp"),
        P("tp", "slot"),
    )
    out_specs = P("slot", "tp")
    return jax.shard_map(
        per_device, mesh=mesh, in_specs=in_specs, out_specs=out_specs, check_vma=False
    )
```

```python
import math

import jax
import jax.numpy as jnp
from jax import lax
from jax.experimental import pallas as pl
from jax.experimental.pallas import tpu as pltpu
from jax.sharding import PartitionSpec as P

HD = 128
BLK = 16
NX, NZ, NY = 4, 8, 4
RING = (4, 3, 5, 2, 6, 1, 7)
MESH = pl.DeviceIdType.MESH
BF = jnp.bfloat16
F32 = jnp.float32
NEG = -1e30
NT = (((1,), (1,)), ((), ()))
VM = pltpu.VMEM
DMA = pltpu.SemaphoreType.DMA


def remote(src, dst, ssem, rsem, **where):
    return pltpu.make_async_remote_copy(
        src_ref=src, dst_ref=dst, send_sem=ssem, recv_sem=rsem, device_id=where, device_id_type=MESH
    )


def loop(lo, hi, body):
    def step(i, c):
        body(i)
        return c

    lax.fori_loop(lo, hi, step, 0)


def layer_kernel(
    q_in, kn_in, vn_in, kc, vc, wt, lists, counts, res_in,
    out,
    q, kn, vn, resid, ins,
    sk, sv, kb, vb, rk, rv, wz, ws, seen, mx, tot, acc, tab, tabs,
    a, part, got, red, fin, flat,
    ts, k1s, k1r, k2s, k2r, v1s, v1r, v2s, v2r, os, orr, w1s, w1r, wps, wpr, wms, wmr, wcs, wcr,
    cs, cr, a1s, a1r, a2s, a2r, ys, yr, hs, hr,
):
    me = lax.axis_index("slot")
    tp = lax.axis_index("tp")
    x, z, y, core = me // NZ, me % NZ, tp // 2, tp % 2
    sib = tp + 1 - 2 * core
    left, right, across = (x + 3) % NX, (x + 1) % NX, (x + 2) % NX
    heads = q.shape[1] // HD
    c2 = math.log2(math.e) / math.sqrt(HD)

    def at(ax, az):
        return ax * NZ + az

    def put(src, dst, ssem, rsem, **where):
        remote(src, dst, ssem, rsem, **where).start()

    def take(dst, rsem):
        remote(dst, dst, rsem, rsem, slot=me).wait_recv()

    def sent(src, ssem):
        remote(src, src, ssem, ssem, slot=me).wait_send()

    barrier = pltpu.get_barrier_semaphore()
    for d in range(1, NX):
        pl.semaphore_signal(barrier, inc=1, device_id={"slot": at((x + d) % NX, z)}, device_id_type=MESH)
    for d in range(1, NZ):
        pl.semaphore_signal(barrier, inc=1, device_id={"slot": at(x, (z + d) % NZ)}, device_id_type=MESH)
    for d in range(1, NY):
        pl.semaphore_signal(barrier, inc=1, device_id={"tp": ((y + d) % NY) * 2 + core}, device_id_type=MESH)
    pl.semaphore_signal(barrier, inc=1, device_id={"tp": sib}, device_id_type=MESH)

    fetch = [
        pltpu.make_async_copy(src, dst, ins.at[i])
        for i, (src, dst) in enumerate(((q_in, q), (kn_in, kn), (vn_in, vn), (res_in, resid)))
    ]
    for copy in fetch:
        copy.start()

    lst = lists[...]
    readers = lst.shape[0]
    sub = lax.broadcasted_iota(jnp.int32, (readers, 128), 0)
    lane = lax.broadcasted_iota(jnp.int32, (readers, 128), 1)
    live_n = jnp.sum(jnp.where(sub[:, :readers] == lane[:, :readers], counts[...], 0), 1, keepdims=True)
    live = lax.broadcasted_iota(jnp.int32, lst.shape, 1) < live_n
    mine = live & (lst // BLK == me)
    within = lst % BLK
    lo = jnp.min(jnp.where(mine, within, BLK), 1, keepdims=True)
    hi = jnp.max(jnp.where(mine, within, 0), 1, keepdims=True)
    lo = jnp.where(lo < BLK, lo, 0)
    tab[0:1, :] = jnp.sum(jnp.where(sub == lane, lo, 0), 0, keepdims=True)
    tab[1:2, :] = jnp.sum(jnp.where(sub == lane, hi, 0), 0, keepdims=True)
    to_scalar = pltpu.make_async_copy(tab, tabs, ts)
    to_scalar.start()

    row = lists[pl.ds(me, 1), :]
    n_live = jnp.sum(jnp.where(lax.broadcasted_iota(jnp.int32, counts.shape, 1) == me, counts[...], 0), 1, keepdims=True)
    row_live = lax.broadcasted_iota(jnp.int32, row.shape, 1) < n_live
    owner = lax.broadcasted_iota(jnp.int32, lst.shape, 0)
    n_of = jnp.sum(jnp.where((row // BLK == owner) & row_live, 1, 0), 1, keepdims=True)
    for x1 in range(NX):
        key = lax.broadcasted_iota(jnp.int32, (readers, 256), 1)
        own_of = lax.broadcasted_iota(jnp.int32, (readers, 256), 0)
        cnt = jnp.sum(jnp.where(own_of == x1 * NZ + key // 32, n_of, 0), 0, keepdims=True)
        odd = (lax.broadcasted_iota(jnp.int32, (1, 256), 1) // BLK) % 2
        seen[x1] = jnp.broadcast_to(jnp.where(cnt > odd, 1.0, 0.0), (8, 256))
    to_scalar.wait()

    def pack(x2):
        for z2 in range(NZ):
            r = at(x2, z2)
            for half in range(2):
                blk = tabs[half, r]
                sk[x2, z2, half * BLK : (half + 1) * BLK, :] = kc[blk]
                sv[x2, z2, half * BLK : (half + 1) * BLK, :] = vc[blk]

    pack(x)
    pl.semaphore_wait(barrier, NX - 1 + NZ - 1 + NY - 1 + 1)

    for d in RING:
        z2 = (z + d) % NZ

        @pl.when(z2 > z)
        def _():
            put(sk.at[x, z2], rk.at[x, z], os.at[z2], orr.at[z], slot=at(x, z2))
            put(sv.at[x, z2], rv.at[x, z], os.at[z2], orr.at[z], slot=at(x, z2))

    def give(x2):
        pack(x2)
        for d in RING:
            z2 = (z + d) % NZ
            put(sv.at[x2, z2], vb.at[x2, z], v1s.at[x2], v1r.at[x2, z], slot=at(x, z2))
            put(sk.at[x2, z2], kb.at[x, z2], k1s.at[x2], k1r.at[x, z2], slot=at(x2, z))
        put(sk.at[x2, z], rk.at[x, z], k1s.at[x2], k2r.at[x], slot=at(x2, z))
        put(sv.at[x2, z], rv.at[x, z], v1s.at[x2], v2r.at[x], slot=at(x2, z))

    loop(x + 1, NX, give)
    for d in (1, 3, 2):
        x2 = (x + d) % NX
        put(wt.at[x2], wz.at[z, x], w1s.at[x2], w1r.at[x], slot=at(x2, z))
    mine_w = pltpu.make_async_copy(wt.at[x], wz.at[z, x], ins.at[4])
    mine_w.start()

    def blank(z1):
        rk[x, z1] = jnp.zeros(rk.shape[2:], BF)
        rv[x, z1] = jnp.zeros(rv.shape[2:], BF)

    loop(z, NZ, blank)

    for copy in fetch:
        copy.wait()
    mine_w.wait()
    for h in range(heads):
        cols = slice(h * HD, (h + 1) * HD)
        s = lax.dot_general(q[:, cols], kn[:, cols], NT, preferred_element_type=F32)
        top = jnp.broadcast_to(jnp.max(s, 1, keepdims=True), (256, HD))
        p = jnp.exp2((s - jnp.concatenate([top, top], 1)) * c2)
        mx[h] = top
        tot[h] = jnp.broadcast_to(jnp.sum(p, 1, keepdims=True), (256, HD))
        acc[:, cols] = jnp.dot(p.astype(BF), vn[:, cols], preferred_element_type=F32)

    def chunk(x1):
        ok = seen[x1][0:1, :] > 0.5
        for h in range(heads):
            cols = slice(h * HD, (h + 1) * HD)
            keys = rk[x1, :, :, cols].reshape(256, HD)
            vals = rv[x1, :, :, cols].reshape(256, HD)
            s = lax.dot_general(q[:, cols], keys, NT, preferred_element_type=F32)
            s = jnp.where(ok, s, NEG)
            old = mx[h]
            top = jnp.maximum(old, jnp.max(s, 1, keepdims=True))
            fade = jnp.exp2((old - top) * c2)
            p = jnp.exp2((s - jnp.concatenate([top, top], 1)) * c2)
            mx[h] = top
            tot[h] = tot[h] * fade + jnp.sum(p, 1, keepdims=True)
            acc[:, cols] = acc[:, cols] * fade + jnp.dot(p.astype(BF), vals, preferred_element_type=F32)

    def w_pass(zs, sem):
        @pl.when(zs // 4 != core)
        def _():
            put(wz.at[zs], ws.at[zs % 4], wcs.at[zs % 4], wcr.at[zs % 4], tp=sib)

    def ring_step(k):
        zp, zm = (z + 1) % NZ, (z + NZ - 1) % NZ
        up, dn = (z + NZ - k + 1) % NZ, (z + k - 1) % NZ
        if k == 1:
            for d in (1, 3, 2):
                x1 = (x + d) % NX
                take(wz.at[z, x1], w1r.at[x1])
        if k > 1:
            take(wz.at[up], wpr.at[k - 2])
            take(wz.at[dn], wmr.at[k - 2])
        if k < 4:
            put(wz.at[up], wz.at[up], wps.at[k - 1], wpr.at[k - 1], slot=at(x, zp))
            put(wz.at[dn], wz.at[dn], wms.at[k - 1], wmr.at[k - 1], slot=at(x, zm))
        else:
            put(wz.at[up, pl.ds(0, 2)], wz.at[up, pl.ds(0, 2)], wps.at[3], wpr.at[3], slot=at(x, zp))
            put(wz.at[dn, pl.ds(2, 2)], wz.at[dn, pl.ds(2, 2)], wms.at[3], wmr.at[3], slot=at(x, zm))
        w_pass(up, 0)
        if k > 1:
            w_pass(dn, 0)

    def fwd_k(i):
        x1 = x - 1 - i
        for d in RING:
            z2 = (z + d) % NZ
            take(kb.at[x1, z2], k1r.at[x1, z2])
            put(kb.at[x1, z2], rk.at[x1, z], k2s.at[x1], k2r.at[x1], slot=at(x, z2))

    loop(0, x, fwd_k)

    def own_row(z1):
        take(vb.at[0, pl.ds(0, 2)], orr.at[z1])

    loop(0, z, own_row)
    chunk(x)

    for i, d in enumerate(RING):
        z2 = (z + d) % NZ

        def fwd_v(x2):
            take(vb.at[x2, z2], v1r.at[x2, z2])
            put(vb.at[x2, z2], rv.at[x, z2], v2s.at[x2], v2r.at[x], slot=at(x2, z))

        loop(x + 1, NX, fwd_v)
        if i == 3:
            ring_step(1)
    ring_step(2)

    def earlier(i):
        x1 = x - 1 - i
        take(rk.at[x1], k2r.at[x1])
        take(rv.at[x1], v2r.at[x1])
        chunk(x1)

    loop(0, x, earlier)
    for h in range(heads):
        cols = slice(h * HD, (h + 1) * HD)
        a[core, x, :, cols] = (acc[:, cols] / tot[h]).astype(BF)

    def rows(c, g, r):
        return a.at[c, g, pl.ds(r * 128, 128)]

    def to_sib(g, r):
        put(rows(core, g, r), rows(core, g, r), cs.at[g, r], cr.at[g, r], tp=sib)

    def from_sib(g, r):
        take(rows(1 - core, g, r), cr.at[g, r])

    for r in range(2):
        put(rows(core, x, r), rows(core, x, r), a1s.at[0, r], a1r.at[0, r], slot=at(right, z))
        put(rows(core, x, 1 - r), rows(core, x, 1 - r), a1s.at[1, 1 - r], a1r.at[1, 1 - r], slot=at(left, z))
    to_sib(x, 0)
    to_sib(x, 1)

    def tile(g, zl, r, n):
        zs = core * 4 + zl
        o = lax.dot_general(wz[zs].reshape(192, 768), a[core, g, pl.ds(r * 128, n * 128)], NT, preferred_element_type=F32)
        o += lax.dot_general(ws[zl].reshape(192, 768), a[1 - core, g, pl.ds(r * 128, n * 128)], NT, preferred_element_type=F32)
        for i in range(n):
            for p in range(NY):
                part[g, r + i, p, zl] = o[p * 48 : (p + 1) * 48, i * 128 : (i + 1) * 128].astype(BF)
            for d in (1, 3, 2):
                p = (y + d) % NY
                put(
                    part.at[g, r + i, p, zl], got.at[g, r + i, y, zl],
                    ys.at[g], yr.at[g, r + i], tp=p * 2 + core,
                )

    def tiles(g, r, n, k0, k1):
        def one(k):
            d = (k % 2) * ((k + 1) // 2) + (1 - k % 2) * ((NZ - k // 2) % NZ)
            zs = (z + d) % NZ

            @pl.when(zs // 4 == core)
            def _():
                tile(g, zs % 4, r, n)

        loop(k0, k1, one)

    def w_here(k0, k1):
        def one(k):
            d = (k % 2) * ((k + 1) // 2) + (1 - k % 2) * ((NZ - k // 2) % NZ)
            zs = (z + d) % NZ

            @pl.when(zs // 4 == core)
            def _():
                take(ws.at[zs % 4], wcr.at[zs % 4])

        loop(k0, k1, one)

    def half_in(i):
        if i == 0:
            take(rows(core, left, 0), a1r.at[0, 0])
            put(rows(core, left, 0), rows(core, left, 0), a2s.at[0], a2r.at[0], slot=at(right, z))
            to_sib(left, 0)
            take(rows(core, right, 1), a1r.at[1, 1])
            put(rows(core, right, 1), rows(core, right, 1), a2s.at[1], a2r.at[1], slot=at(left, z))
            to_sib(right, 1)
        else:
            take(rows(core, left, 1), a1r.at[0, 1])
            to_sib(left, 1)
            take(rows(core, right, 0), a1r.at[1, 0])
            to_sib(right, 0)

    for r in range(2):
        from_sib(x, r)
    w_here(0, 3)
    tiles(x, 0, 2, 0, 3)
    half_in(0)
    ring_step(3)
    w_here(3, 5)
    tiles(x, 0, 2, 3, 5)
    from_sib(left, 0)
    tiles(left, 0, 1, 0, 5)
    from_sib(right, 1)
    tiles(right, 1, 1, 0, 5)
    half_in(1)
    from_sib(left, 1)
    tiles(left, 1, 1, 0, 5)
    from_sib(right, 0)
    tiles(right, 0, 1, 0, 5)
    ring_step(4)
    w_here(5, 7)
    tiles(x, 0, 2, 5, 7)
    tiles(left, 0, 2, 5, 7)
    tiles(right, 0, 2, 5, 7)
    take(rows(core, across, 0), a2r.at[0])
    to_sib(across, 0)
    take(rows(core, across, 1), a2r.at[1])
    to_sib(across, 1)
    for r in range(2):
        from_sib(across, r)
    tiles(across, 0, 2, 0, 7)
    far = (z + 4) % NZ
    take(wz.at[far, pl.ds(0, 2)], wpr.at[3])
    take(wz.at[far, pl.ds(2, 2)], wmr.at[3])
    w_pass(far, 0)
    w_here(7, 8)
    for g in (across, left, right, x):
        tiles(g, 0, 2, 7, 8)

    def reduce(g, r):
        take(got.at[g, r, pl.ds(0, 3)], yr.at[g, r])
        s = part[g, r, y].astype(F32)
        for d in (1, 3, 2):
            src = (y + NY - d) % NY
            s += got[g, r, src].astype(F32)
        return s.astype(BF)

    for d in (3, 1, 2):
        g = (x + d) % NX
        for r in range(2):
            red[g, r] = reduce(g, r)
        put(red.at[g], fin.at[x], hs.at[d - 1], hr.at[d - 1], slot=at(g, z))
    for r in range(2):
        fin[x, r] = reduce(x, r)
    for d in (3, 1, 2):
        take(fin.at[(x + NX - d) % NX], hr.at[d - 1])
    for src in range(NX):
        for zs in range(4):
            for r in range(2):
                flat[zs * 192 + src * 48 : zs * 192 + (src + 1) * 48, r * 128 : (r + 1) * 128] = fin[src, r, zs]
    sub = lax.broadcasted_iota(jnp.int32, (256, 256), 0)
    lane = lax.broadcasted_iota(jnp.int32, (256, 256), 1)
    eye = jnp.where(sub == lane, 1.0, 0.0).astype(BF)
    summed = lax.dot_general(eye, flat[...], NT, preferred_element_type=F32)
    out[...] = (resid[...].astype(F32) + summed).astype(BF)

    for d in (1, 3, 2):
        x2 = (x + d) % NX
        sent(wt.at[x2], w1s.at[x2])
        sent(red.at[x2], hs.at[d - 1])
    for k in range(3):
        sent(wz.at[z], wps.at[k])
        sent(wz.at[z], wms.at[k])
    sent(wz.at[z, pl.ds(0, 2)], wps.at[3])
    sent(wz.at[z, pl.ds(2, 2)], wms.at[3])
    for zl in range(4):
        sent(wz.at[z], wcs.at[zl])
    for r in range(2):
        for g in range(NX):
            sent(rows(core, x, r), cs.at[g, r])
        for i in range(2):
            sent(rows(core, x, r), a1s.at[i, r])
        sent(rows(core, x, r), a2s.at[r])

    for g in range(NX):
        sent(part.at[g, pl.ds(0, 2), pl.ds(0, 3)], ys.at[g])

    def row_sent(z2):
        sent(sk.at[x, pl.ds(0, 2)], os.at[z2])

    def given(x2):
        sent(sk.at[x2], k1s.at[x2])
        sent(sv.at[x2], v1s.at[x2])
        sent(vb.at[x2, pl.ds(0, NZ - 1)], v2s.at[x2])

    def passed(x1):
        sent(kb.at[x1, pl.ds(0, NZ - 1)], k2s.at[x1])

    loop(z + 1, NZ, row_sent)
    loop(x + 1, NX, given)
    loop(0, x, passed)


def per_device(queries, k_new, v_new, k_clean, v_clean, lists, counts, resid, w_out):
    width = queries.shape[1]
    wt = w_out.T.reshape(NX, 48, width)
    blocks = (-1, BLK, width)
    vm, hbm = pl.BlockSpec(memory_space=VM), pl.BlockSpec(memory_space=pl.ANY)
    heads = width // HD
    return pl.pallas_call(
        layer_kernel,
        out_shape=jax.ShapeDtypeStruct((256, width), BF),
        in_specs=[hbm] * 3 + [vm] * 2 + [hbm] + [vm] * 2 + [hbm],
        out_specs=vm,
        scratch_shapes=[
            VM((256, width), BF), VM((256, width), BF), VM((256, width), BF), VM((256, width), BF), DMA((5,)),
            VM((NX, NZ, 32, width), BF), VM((NX, NZ, 32, width), BF),
            VM((NX, NZ, 32, width), BF), VM((NX, NZ, 32, width), BF),
            VM((NX, NZ, 32, width), BF), VM((NX, NZ, 32, width), BF),
            VM((NZ, NX, 48, width), BF), VM((4, NX, 48, width), BF), VM((NX, 8, 256), F32),
            VM((heads, 256, HD), F32), VM((heads, 256, HD), F32), VM((256, width), F32),
            VM((8, 128), jnp.int32), pltpu.SMEM((8, 128), jnp.int32),
            VM((2, NX, 256, width), BF), VM((NX, 2, NY, 4, 48, 128), BF), VM((NX, 2, NY, 4, 48, 128), BF),
            VM((NX, 2, 4, 48, 128), BF), VM((NX, 2, 4, 48, 128), BF), VM((width, 256), BF),
            DMA, DMA((NX,)), DMA((NX, NZ)), DMA((NX,)), DMA((NX,)),
            DMA((NX,)), DMA((NX, NZ)), DMA((NX,)), DMA((NX,)),
            DMA((NZ,)), DMA((NZ,)), DMA((NX,)), DMA((NX,)),
            DMA((4,)), DMA((4,)), DMA((4,)), DMA((4,)), DMA((4,)), DMA((4,)),
            DMA((NX, 2)), DMA((NX, 2)), DMA((2, 2)), DMA((2, 2)), DMA((2,)), DMA((2,)),
            DMA((NX,)), DMA((NX, 2)), DMA((3,)), DMA((3,)),
        ],
        compiler_params=pltpu.CompilerParams(
            collective_id=0, has_side_effects=True, vmem_limit_bytes=56 << 20
        ),
        name="layer",
    )(
        queries, k_new, v_new, k_clean.reshape(blocks), v_clean.reshape(blocks), wt,
        lists, counts.reshape(1, -1), resid,
    )


def solution(mesh):
    in_specs = (
        P("slot", "tp"),
        P("slot", "tp"),
        P("slot", "tp"),
        P("slot", "tp"),
        P("slot", "tp"),
        P(),
        P(),
        P("slot", "tp"),
        P("tp", "slot"),
    )
    out_specs = P("slot", "tp")
    return jax.shard_map(
        per_device, mesh=mesh, in_specs=in_specs, out_specs=out_specs, check_vma=False
    )
```

```python
import functools
import math

import jax
import jax.numpy as jnp
from jax import lax
from jax.experimental import pallas as pl
from jax.experimental.pallas import tpu as pltpu
from jax.sharding import PartitionSpec as P

HD = 128
BLK = 16
NX, NZ, NY = 4, 8, 4
FAR, NEAR = (4, 3, 5), (2, 6, 1, 7)
MESH = pl.DeviceIdType.MESH
BF = jnp.bfloat16
F32 = jnp.float32
NEG = -1e30
NT = (((1,), (1,)), ((), ()))
VM = pltpu.VMEM
DMA = pltpu.SemaphoreType.DMA


def remote(src, dst, ssem, rsem, **where):
    return pltpu.make_async_remote_copy(
        src_ref=src, dst_ref=dst, send_sem=ssem, recv_sem=rsem, device_id=where, device_id_type=MESH
    )


def loop(lo, hi, body):
    def step(i, c):
        body(i)
        return c

    lax.fori_loop(lo, hi, step, 0)


def layer_kernel(
    q_in, kn_in, vn_in, kc_in, vc_in, wt, lists, counts, res_in,
    out,
    q, kn, vn, resid, kc, vc, ins,
    sk, sv, kb, vb, rk, rv, wz, ws, seen, mx, tot, acc, tab, tabs,
    a, part, got, red, fin, flat,
    ts, k1s, k1r, k2s, k2r, v1s, v1r, v2s, v2r, os, orr, w1s, w1r, wps, wpr, wms, wmr, wcs, wcr,
    cs, cr, a1s, a1r, a2s, a2r, ys, yr, hs, hr,
):
    me = lax.axis_index("slot")
    tp = lax.axis_index("tp")
    x, z, y, core = me // NZ, me % NZ, tp // 2, tp % 2
    sib = tp + 1 - 2 * core
    left, right, across = (x + 3) % NX, (x + 1) % NX, (x + 2) % NX
    heads = q.shape[1] // HD
    c2 = math.log2(math.e) / math.sqrt(HD)

    def at(ax, az):
        return ax * NZ + az

    def put(src, dst, ssem, rsem, **where):
        remote(src, dst, ssem, rsem, **where).start()

    def take(dst, rsem):
        remote(dst, dst, rsem, rsem, slot=me).wait_recv()

    def sent(src, ssem):
        remote(src, src, ssem, ssem, slot=me).wait_send()

    barrier = pltpu.get_barrier_semaphore()
    for d in range(1, NX):
        pl.semaphore_signal(barrier, inc=1, device_id={"slot": at((x + d) % NX, z)}, device_id_type=MESH)
    for d in range(1, NZ):
        pl.semaphore_signal(barrier, inc=1, device_id={"slot": at(x, (z + d) % NZ)}, device_id_type=MESH)
    for d in range(1, NY):
        pl.semaphore_signal(barrier, inc=1, device_id={"tp": ((y + d) % NY) * 2 + core}, device_id_type=MESH)
    pl.semaphore_signal(barrier, inc=1, device_id={"tp": sib}, device_id_type=MESH)

    blocks = [pltpu.make_async_copy(kc_in, kc, ins.at[5]), pltpu.make_async_copy(vc_in, vc, ins.at[6])]
    for copy in blocks:
        copy.start()
    fetch = [
        pltpu.make_async_copy(src, dst, ins.at[i])
        for i, (src, dst) in enumerate(((q_in, q), (kn_in, kn), (vn_in, vn), (res_in, resid)))
    ]
    for copy in fetch:
        copy.start()

    lst = lists[...]
    readers = lst.shape[0]
    sub = lax.broadcasted_iota(jnp.int32, (readers, 128), 0)
    lane = lax.broadcasted_iota(jnp.int32, (readers, 128), 1)
    live_n = jnp.sum(jnp.where(sub[:, :readers] == lane[:, :readers], counts[...], 0), 1, keepdims=True)
    live = lax.broadcasted_iota(jnp.int32, lst.shape, 1) < live_n
    mine = live & (lst // BLK == me)
    within = lst % BLK
    lo = jnp.min(jnp.where(mine, within, BLK), 1, keepdims=True)
    hi = jnp.max(jnp.where(mine, within, 0), 1, keepdims=True)
    lo = jnp.where(lo < BLK, lo, 0)
    tab[0:1, :] = jnp.sum(jnp.where(sub == lane, lo, 0), 0, keepdims=True)
    tab[1:2, :] = jnp.sum(jnp.where(sub == lane, hi, 0), 0, keepdims=True)
    to_scalar = pltpu.make_async_copy(tab, tabs, ts)
    to_scalar.start()

    row = lists[pl.ds(me, 1), :]
    n_live = jnp.sum(jnp.where(lax.broadcasted_iota(jnp.int32, counts.shape, 1) == me, counts[...], 0), 1, keepdims=True)
    row_live = lax.broadcasted_iota(jnp.int32, row.shape, 1) < n_live
    owner = lax.broadcasted_iota(jnp.int32, lst.shape, 0)
    n_of = jnp.sum(jnp.where((row // BLK == owner) & row_live, 1, 0), 1, keepdims=True)
    for x1 in range(NX):
        key = lax.broadcasted_iota(jnp.int32, (readers, 256), 1)
        own_of = lax.broadcasted_iota(jnp.int32, (readers, 256), 0)
        cnt = jnp.sum(jnp.where(own_of == x1 * NZ + key // 32, n_of, 0), 0, keepdims=True)
        odd = (lax.broadcasted_iota(jnp.int32, (1, 256), 1) // BLK) % 2
        seen[x1] = jnp.broadcast_to(jnp.where(cnt > odd, 1.0, 0.0), (8, 256))
    to_scalar.wait()

    def pack(x2):
        for z2 in range(NZ):
            r = at(x2, z2)
            for half in range(2):
                blk = tabs[half, r]
                sk[x2, z2, half * BLK : (half + 1) * BLK, :] = kc[blk]
                sv[x2, z2, half * BLK : (half + 1) * BLK, :] = vc[blk]

    for copy in blocks:
        copy.wait()
    pack(x)
    pl.semaphore_wait(barrier, NX - 1 + NZ - 1 + NY - 1 + 1)

    def give_row(ds):
        for d in ds:
            z2 = (z + d) % NZ

            @pl.when(z2 > z)
            def _():
                put(sk.at[x, z2], rk.at[x, z], os.at[z2], orr.at[z], slot=at(x, z2))
                put(sv.at[x, z2], rv.at[x, z], os.at[z2], orr.at[z], slot=at(x, z2))

    def give_v(ds, x2):
        for d in ds:
            z2 = (z + d) % NZ
            put(sv.at[x2, z2], vb.at[x2, z], v1s.at[x2], v1r.at[x2, z], slot=at(x, z2))

    def give(x2):
        pack(x2)
        for d in FAR:
            z2 = (z + d) % NZ
            put(sv.at[x2, z2], vb.at[x2, z], v1s.at[x2], v1r.at[x2, z], slot=at(x, z2))
            put(sk.at[x2, z2], kb.at[x, z2], k1s.at[x2], k1r.at[x, z2], slot=at(x2, z))

    def give_k(x2):
        for d in NEAR:
            z2 = (z + d) % NZ
            put(sk.at[x2, z2], kb.at[x, z2], k1s.at[x2], k1r.at[x, z2], slot=at(x2, z))
        put(sk.at[x2, z], rk.at[x, z], k1s.at[x2], k2r.at[x], slot=at(x2, z))

    def give_rest(x2):
        put(sv.at[x2, z], rv.at[x, z], v1s.at[x2], v2r.at[x], slot=at(x2, z))

    give_row(FAR)
    loop(x + 1, NX, give)
    loop(x + 1, NX, give_k)
    for d in (1, 3, 2):
        x2 = (x + d) % NX
        put(wt.at[x2], wz.at[z, x], w1s.at[x2], w1r.at[x], slot=at(x2, z))
    mine_w = pltpu.make_async_copy(wt.at[x], wz.at[z, x], ins.at[4])
    mine_w.start()

    def blank(z1):
        rk[x, z1] = jnp.zeros(rk.shape[2:], BF)
        rv[x, z1] = jnp.zeros(rv.shape[2:], BF)

    loop(z, NZ, blank)

    for copy in fetch:
        copy.wait()
    mine_w.wait()
    for h in range(heads):
        cols = slice(h * HD, (h + 1) * HD)
        s = lax.dot_general(q[:, cols], kn[:, cols], NT, preferred_element_type=F32)
        top = jnp.broadcast_to(jnp.max(s, 1, keepdims=True), (256, HD))
        p = jnp.exp2((s - jnp.concatenate([top, top], 1)) * c2)
        mx[h] = top
        tot[h] = jnp.broadcast_to(jnp.sum(p, 1, keepdims=True), (256, HD))
        acc[:, cols] = jnp.dot(p.astype(BF), vn[:, cols], preferred_element_type=F32)

    def chunk(x1):
        ok = seen[x1][0:1, :] > 0.5
        for h in range(heads):
            cols = slice(h * HD, (h + 1) * HD)
            keys = rk[x1, :, :, cols].reshape(256, HD)
            vals = rv[x1, :, :, cols].reshape(256, HD)
            s = lax.dot_general(q[:, cols], keys, NT, preferred_element_type=F32)
            s = jnp.where(ok, s, NEG)
            old = mx[h]
            top = jnp.maximum(old, jnp.max(s, 1, keepdims=True))
            fade = jnp.exp2((old - top) * c2)
            p = jnp.exp2((s - jnp.concatenate([top, top], 1)) * c2)
            mx[h] = top
            tot[h] = tot[h] * fade + jnp.sum(p, 1, keepdims=True)
            acc[:, cols] = acc[:, cols] * fade + jnp.dot(p.astype(BF), vals, preferred_element_type=F32)

    def w_pass(zs, sem):
        @pl.when(zs // 4 != core)
        def _():
            put(wz.at[zs], ws.at[zs % 4], wcs.at[zs % 4], wcr.at[zs % 4], tp=sib)

    def ring_step(k):
        zp, zm = (z + 1) % NZ, (z + NZ - 1) % NZ
        up, dn = (z + NZ - k + 1) % NZ, (z + k - 1) % NZ
        if k == 1:
            for d in (1, 3, 2):
                x1 = (x + d) % NX
                take(wz.at[z, x1], w1r.at[x1])
        if k > 1:
            take(wz.at[up], wpr.at[k - 2])
            take(wz.at[dn], wmr.at[k - 2])
        if k < 4:
            put(wz.at[up], wz.at[up], wps.at[k - 1], wpr.at[k - 1], slot=at(x, zp))
            put(wz.at[dn], wz.at[dn], wms.at[k - 1], wmr.at[k - 1], slot=at(x, zm))
        else:
            put(wz.at[up, pl.ds(0, 2)], wz.at[up, pl.ds(0, 2)], wps.at[3], wpr.at[3], slot=at(x, zp))
            put(wz.at[dn, pl.ds(2, 2)], wz.at[dn, pl.ds(2, 2)], wms.at[3], wmr.at[3], slot=at(x, zm))
        w_pass(up, 0)
        if k > 1:
            w_pass(dn, 0)

    def fwd_k(ds, i):
        x1 = x - 1 - i
        for d in ds:
            z2 = (z + d) % NZ
            take(kb.at[x1, z2], k1r.at[x1, z2])
            put(kb.at[x1, z2], rk.at[x1, z], k2s.at[x1], k2r.at[x1], slot=at(x, z2))

    give_row(NEAR)
    loop(x + 1, NX, functools.partial(give_v, NEAR))
    loop(x + 1, NX, give_rest)
    loop(0, x, functools.partial(fwd_k, FAR))
    loop(0, x, functools.partial(fwd_k, NEAR))

    def own_row(z1):
        take(vb.at[0, pl.ds(0, 2)], orr.at[z1])

    loop(0, z, own_row)
    chunk(x)

    for i, d in enumerate(FAR + NEAR):
        z2 = (z + d) % NZ

        def fwd_v(x2):
            take(vb.at[x2, z2], v1r.at[x2, z2])
            put(vb.at[x2, z2], rv.at[x, z2], v2s.at[x2], v2r.at[x], slot=at(x2, z))

        loop(x + 1, NX, fwd_v)
        if i == 2:
            ring_step(1)
    ring_step(2)

    def earlier(i):
        x1 = x - 1 - i
        take(rk.at[x1], k2r.at[x1])
        take(rv.at[x1], v2r.at[x1])
        chunk(x1)

    loop(0, x, earlier)
    for h in range(heads):
        cols = slice(h * HD, (h + 1) * HD)
        a[core, x, :, cols] = (acc[:, cols] / tot[h]).astype(BF)

    def rows(c, g, r):
        return a.at[c, g, pl.ds(r * 128, 128)]

    def to_sib(g, r):
        put(rows(core, g, r), rows(core, g, r), cs.at[g, r], cr.at[g, r], tp=sib)

    def from_sib(g, r):
        take(rows(1 - core, g, r), cr.at[g, r])

    for r in range(2):
        put(rows(core, x, r), rows(core, x, r), a1s.at[0, r], a1r.at[0, r], slot=at(right, z))
        put(rows(core, x, 1 - r), rows(core, x, 1 - r), a1s.at[1, 1 - r], a1r.at[1, 1 - r], slot=at(left, z))
    to_sib(x, 0)
    to_sib(x, 1)
    ring_step(3)

    def tile(g, zl, r, n):
        zs = core * 4 + zl
        o = lax.dot_general(wz[zs].reshape(192, 768), a[core, g, pl.ds(r * 128, n * 128)], NT, preferred_element_type=F32)
        o += lax.dot_general(ws[zl].reshape(192, 768), a[1 - core, g, pl.ds(r * 128, n * 128)], NT, preferred_element_type=F32)
        for i in range(n):
            for p in range(NY):
                part[g, r + i, p, zl] = o[p * 48 : (p + 1) * 48, i * 128 : (i + 1) * 128].astype(BF)
            for d in (1, 3, 2):
                p = (y + d) % NY
                put(
                    part.at[g, r + i, p, zl], got.at[g, r + i, y, zl],
                    ys.at[g], yr.at[g, r + i], tp=p * 2 + core,
                )

    def tiles(g, r, n, k0, k1):
        def one(k):
            d = (k % 2) * ((k + 1) // 2) + (1 - k % 2) * ((NZ - k // 2) % NZ)
            zs = (z + d) % NZ

            @pl.when(zs // 4 == core)
            def _():
                tile(g, zs % 4, r, n)

        loop(k0, k1, one)

    def w_here(k0, k1):
        def one(k):
            d = (k % 2) * ((k + 1) // 2) + (1 - k % 2) * ((NZ - k // 2) % NZ)
            zs = (z + d) % NZ

            @pl.when(zs // 4 == core)
            def _():
                take(ws.at[zs % 4], wcr.at[zs % 4])

        loop(k0, k1, one)

    def half_in(i):
        if i == 0:
            take(rows(core, left, 0), a1r.at[0, 0])
            put(rows(core, left, 0), rows(core, left, 0), a2s.at[0], a2r.at[0], slot=at(right, z))
            to_sib(left, 0)
            take(rows(core, right, 1), a1r.at[1, 1])
            put(rows(core, right, 1), rows(core, right, 1), a2s.at[1], a2r.at[1], slot=at(left, z))
            to_sib(right, 1)
        else:
            take(rows(core, left, 1), a1r.at[0, 1])
            to_sib(left, 1)
            take(rows(core, right, 0), a1r.at[1, 0])
            to_sib(right, 0)

    for r in range(2):
        from_sib(x, r)
    w_here(0, 3)
    tiles(x, 0, 2, 0, 3)
    half_in(0)
    w_here(3, 5)
    tiles(x, 0, 2, 3, 5)
    from_sib(left, 0)
    tiles(left, 0, 1, 0, 5)
    from_sib(right, 1)
    tiles(right, 1, 1, 0, 5)
    half_in(1)
    from_sib(left, 1)
    tiles(left, 1, 1, 0, 5)
    from_sib(right, 0)
    tiles(right, 0, 1, 0, 5)
    ring_step(4)
    w_here(5, 7)
    tiles(x, 0, 2, 5, 7)
    tiles(left, 0, 2, 5, 7)
    tiles(right, 0, 2, 5, 7)
    take(rows(core, across, 0), a2r.at[0])
    to_sib(across, 0)
    take(rows(core, across, 1), a2r.at[1])
    to_sib(across, 1)
    for r in range(2):
        from_sib(across, r)
    tiles(across, 0, 2, 0, 7)
    far = (z + 4) % NZ
    take(wz.at[far, pl.ds(0, 2)], wpr.at[3])
    take(wz.at[far, pl.ds(2, 2)], wmr.at[3])
    w_pass(far, 0)
    w_here(7, 8)
    for g in (across, left, right, x):
        tiles(g, 0, 2, 7, 8)

    def reduce(g, r):
        take(got.at[g, r, pl.ds(0, 3)], yr.at[g, r])
        s = part[g, r, y].astype(F32)
        for d in (1, 3, 2):
            src = (y + NY - d) % NY
            s += got[g, r, src].astype(F32)
        return s.astype(BF)

    for d in (3, 1, 2):
        g = (x + d) % NX
        for r in range(2):
            red[g, r] = reduce(g, r)
        put(red.at[g], fin.at[x], hs.at[d - 1], hr.at[d - 1], slot=at(g, z))
    for r in range(2):
        fin[x, r] = reduce(x, r)
    for d in (3, 1, 2):
        take(fin.at[(x + NX - d) % NX], hr.at[d - 1])
    for src in range(NX):
        for zs in range(4):
            for r in range(2):
                flat[zs * 192 + src * 48 : zs * 192 + (src + 1) * 48, r * 128 : (r + 1) * 128] = fin[src, r, zs]
    sub = lax.broadcasted_iota(jnp.int32, (256, 256), 0)
    lane = lax.broadcasted_iota(jnp.int32, (256, 256), 1)
    eye = jnp.where(sub == lane, 1.0, 0.0).astype(BF)
    summed = lax.dot_general(eye, flat[...], NT, preferred_element_type=F32)
    out[...] = (resid[...].astype(F32) + summed).astype(BF)

    for d in (1, 3, 2):
        x2 = (x + d) % NX
        sent(wt.at[x2], w1s.at[x2])
        sent(red.at[x2], hs.at[d - 1])
    for k in range(3):
        sent(wz.at[z], wps.at[k])
        sent(wz.at[z], wms.at[k])
    sent(wz.at[z, pl.ds(0, 2)], wps.at[3])
    sent(wz.at[z, pl.ds(2, 2)], wms.at[3])
    for zl in range(4):
        sent(wz.at[z], wcs.at[zl])
    for r in range(2):
        for g in range(NX):
            sent(rows(core, x, r), cs.at[g, r])
        for i in range(2):
            sent(rows(core, x, r), a1s.at[i, r])
        sent(rows(core, x, r), a2s.at[r])

    for g in range(NX):
        sent(part.at[g, pl.ds(0, 2), pl.ds(0, 3)], ys.at[g])

    def row_sent(z2):
        sent(sk.at[x, pl.ds(0, 2)], os.at[z2])

    def given(x2):
        sent(sk.at[x2], k1s.at[x2])
        sent(sv.at[x2], v1s.at[x2])
        sent(vb.at[x2, pl.ds(0, NZ - 1)], v2s.at[x2])

    def passed(x1):
        sent(kb.at[x1, pl.ds(0, NZ - 1)], k2s.at[x1])

    loop(z + 1, NZ, row_sent)
    loop(x + 1, NX, given)
    loop(0, x, passed)


def per_device(queries, k_new, v_new, k_clean, v_clean, lists, counts, resid, w_out):
    width = queries.shape[1]
    wt = w_out.T.reshape(NX, 48, width)
    blocks = (-1, BLK, width)
    vm, hbm = pl.BlockSpec(memory_space=VM), pl.BlockSpec(memory_space=pl.ANY)
    heads = width // HD
    return pl.pallas_call(
        layer_kernel,
        out_shape=jax.ShapeDtypeStruct((256, width), BF),
        in_specs=[hbm] * 6 + [vm] * 2 + [hbm],
        out_specs=vm,
        scratch_shapes=[
            VM((256, width), BF), VM((256, width), BF), VM((256, width), BF), VM((256, width), BF),
            VM((256 // BLK, BLK, width), BF), VM((256 // BLK, BLK, width), BF), DMA((7,)),
            VM((NX, NZ, 32, width), BF), VM((NX, NZ, 32, width), BF),
            VM((NX, NZ, 32, width), BF), VM((NX, NZ, 32, width), BF),
            VM((NX, NZ, 32, width), BF), VM((NX, NZ, 32, width), BF),
            VM((NZ, NX, 48, width), BF), VM((4, NX, 48, width), BF), VM((NX, 8, 256), F32),
            VM((heads, 256, HD), F32), VM((heads, 256, HD), F32), VM((256, width), F32),
            VM((8, 128), jnp.int32), pltpu.SMEM((8, 128), jnp.int32),
            VM((2, NX, 256, width), BF), VM((NX, 2, NY, 4, 48, 128), BF), VM((NX, 2, NY, 4, 48, 128), BF),
            VM((NX, 2, 4, 48, 128), BF), VM((NX, 2, 4, 48, 128), BF), VM((width, 256), BF),
            DMA, DMA((NX,)), DMA((NX, NZ)), DMA((NX,)), DMA((NX,)),
            DMA((NX,)), DMA((NX, NZ)), DMA((NX,)), DMA((NX,)),
            DMA((NZ,)), DMA((NZ,)), DMA((NX,)), DMA((NX,)),
            DMA((4,)), DMA((4,)), DMA((4,)), DMA((4,)), DMA((4,)), DMA((4,)),
            DMA((NX, 2)), DMA((NX, 2)), DMA((2, 2)), DMA((2, 2)), DMA((2,)), DMA((2,)),
            DMA((NX,)), DMA((NX, 2)), DMA((3,)), DMA((3,)),
        ],
        compiler_params=pltpu.CompilerParams(
            collective_id=0, has_side_effects=True, vmem_limit_bytes=56 << 20
        ),
        name="layer",
    )(
        queries, k_new, v_new, k_clean.reshape(blocks), v_clean.reshape(blocks), wt,
        lists, counts.reshape(1, -1), resid,
    )


def solution(mesh):
    in_specs = (
        P("slot", "tp"),
        P("slot", "tp"),
        P("slot", "tp"),
        P("slot", "tp"),
        P("slot", "tp"),
        P(),
        P(),
        P("slot", "tp"),
        P("tp", "slot"),
    )
    out_specs = P("slot", "tp")
    return jax.shard_map(
        per_device, mesh=mesh, in_specs=in_specs, out_specs=out_specs, check_vma=False
    )
```

```python
import functools
import math

import jax
import jax.numpy as jnp
from jax import lax
from jax.experimental import pallas as pl
from jax.experimental.pallas import tpu as pltpu
from jax.sharding import PartitionSpec as P

HD = 128
BLK = 16
NX, NZ, NY = 4, 8, 4
FAR, NEAR = (4, 3, 5), (2, 6, 1, 7)
MESH = pl.DeviceIdType.MESH
BF = jnp.bfloat16
F32 = jnp.float32
NEG = -1e30
NT = (((1,), (1,)), ((), ()))
VM = pltpu.VMEM
DMA = pltpu.SemaphoreType.DMA


def remote(src, dst, ssem, rsem, **where):
    return pltpu.make_async_remote_copy(
        src_ref=src, dst_ref=dst, send_sem=ssem, recv_sem=rsem, device_id=where, device_id_type=MESH
    )


def loop(lo, hi, body):
    def step(i, c):
        body(i)
        return c

    lax.fori_loop(lo, hi, step, 0)


def layer_kernel(
    q_in, kn_in, vn_in, kc_in, vc_in, wt, lists, counts, res_in,
    out,
    q, kn, vn, resid, kc, vc, ins,
    sk, sv, kb, vb, rk, rv, wz, ws, seen, mx, tot, acc, tab, tabs,
    a, part, got, red, fin, flat,
    ts, k1s, k1r, k2s, k2r, v1s, v1r, v2s, v2r, os, orr, w1s, w1r, wps, wpr, wms, wmr, wcs, wcr,
    cs, cr, a1s, a1r, a2s, a2r, ys, yr, hs, hr,
):
    me = lax.axis_index("slot")
    tp = lax.axis_index("tp")
    x, z, y, core = me // NZ, me % NZ, tp // 2, tp % 2
    sib = tp + 1 - 2 * core
    left, right, across = (x + 3) % NX, (x + 1) % NX, (x + 2) % NX
    heads = q.shape[1] // HD
    c2 = math.log2(math.e) / math.sqrt(HD)

    def at(ax, az):
        return ax * NZ + az

    def put(src, dst, ssem, rsem, **where):
        remote(src, dst, ssem, rsem, **where).start()

    def take(dst, rsem):
        remote(dst, dst, rsem, rsem, slot=me).wait_recv()

    def sent(src, ssem):
        remote(src, src, ssem, ssem, slot=me).wait_send()

    barrier = pltpu.get_barrier_semaphore()
    for d in range(1, NX):
        pl.semaphore_signal(barrier, inc=1, device_id={"slot": at((x + d) % NX, z)}, device_id_type=MESH)
    for d in range(1, NZ):
        pl.semaphore_signal(barrier, inc=1, device_id={"slot": at(x, (z + d) % NZ)}, device_id_type=MESH)
    for d in range(1, NY):
        pl.semaphore_signal(barrier, inc=1, device_id={"tp": ((y + d) % NY) * 2 + core}, device_id_type=MESH)
    pl.semaphore_signal(barrier, inc=1, device_id={"tp": sib}, device_id_type=MESH)

    blocks = [pltpu.make_async_copy(kc_in, kc, ins.at[5]), pltpu.make_async_copy(vc_in, vc, ins.at[6])]
    for copy in blocks:
        copy.start()
    fetch = [
        pltpu.make_async_copy(src, dst, ins.at[i])
        for i, (src, dst) in enumerate(((q_in, q), (kn_in, kn), (vn_in, vn), (res_in, resid)))
    ]
    for copy in fetch:
        copy.start()

    lst = lists[...]
    readers = lst.shape[0]
    sub = lax.broadcasted_iota(jnp.int32, (readers, 128), 0)
    lane = lax.broadcasted_iota(jnp.int32, (readers, 128), 1)
    live_n = jnp.sum(jnp.where(sub[:, :readers] == lane[:, :readers], counts[...], 0), 1, keepdims=True)
    live = lax.broadcasted_iota(jnp.int32, lst.shape, 1) < live_n
    mine = live & (lst // BLK == me)
    within = lst % BLK
    lo = jnp.min(jnp.where(mine, within, BLK), 1, keepdims=True)
    hi = jnp.max(jnp.where(mine, within, 0), 1, keepdims=True)
    lo = jnp.where(lo < BLK, lo, 0)
    tab[0:1, :] = jnp.sum(jnp.where(sub == lane, lo, 0), 0, keepdims=True)
    tab[1:2, :] = jnp.sum(jnp.where(sub == lane, hi, 0), 0, keepdims=True)
    to_scalar = pltpu.make_async_copy(tab, tabs, ts)
    to_scalar.start()

    row = lists[pl.ds(me, 1), :]
    n_live = jnp.sum(jnp.where(lax.broadcasted_iota(jnp.int32, counts.shape, 1) == me, counts[...], 0), 1, keepdims=True)
    row_live = lax.broadcasted_iota(jnp.int32, row.shape, 1) < n_live
    owner = lax.broadcasted_iota(jnp.int32, lst.shape, 0)
    n_of = jnp.sum(jnp.where((row // BLK == owner) & row_live, 1, 0), 1, keepdims=True)
    for x1 in range(NX):
        key = lax.broadcasted_iota(jnp.int32, (readers, 256), 1)
        own_of = lax.broadcasted_iota(jnp.int32, (readers, 256), 0)
        cnt = jnp.sum(jnp.where(own_of == x1 * NZ + key // 32, n_of, 0), 0, keepdims=True)
        odd = (lax.broadcasted_iota(jnp.int32, (1, 256), 1) // BLK) % 2
        seen[x1] = jnp.broadcast_to(jnp.where(cnt > odd, 1.0, 0.0), (8, 256))
    to_scalar.wait()

    def pack(x2):
        for z2 in range(NZ):
            r = at(x2, z2)
            for half in range(2):
                blk = tabs[half, r]
                sk[x2, z2, half * BLK : (half + 1) * BLK, :] = kc[blk]
                sv[x2, z2, half * BLK : (half + 1) * BLK, :] = vc[blk]

    for copy in blocks:
        copy.wait()
    pack(x)
    pl.semaphore_wait(barrier, NX - 1 + NZ - 1 + NY - 1 + 1)

    def give_row(ds):
        for d in ds:
            z2 = (z + d) % NZ

            @pl.when(z2 > z)
            def _():
                put(sk.at[x, z2], rk.at[x, z], os.at[z2], orr.at[z], slot=at(x, z2))
                put(sv.at[x, z2], rv.at[x, z], os.at[z2], orr.at[z], slot=at(x, z2))

    def give_v(ds, x2):
        for d in ds:
            z2 = (z + d) % NZ
            put(sv.at[x2, z2], vb.at[x2, z], v1s.at[x2], v1r.at[x2, z], slot=at(x, z2))

    def give(x2):
        pack(x2)
        for d in FAR:
            z2 = (z + d) % NZ
            put(sv.at[x2, z2], vb.at[x2, z], v1s.at[x2], v1r.at[x2, z], slot=at(x, z2))
            put(sk.at[x2, z2], kb.at[x, z2], k1s.at[x2], k1r.at[x, 0], slot=at(x2, z))

    def give_k(x2):
        for d in NEAR:
            z2 = (z + d) % NZ
            put(sk.at[x2, z2], kb.at[x, z2], k1s.at[x2], k1r.at[x, 1], slot=at(x2, z))
        put(sk.at[x2, z], rk.at[x, z], k1s.at[x2], k2r.at[x], slot=at(x2, z))

    def give_rest(x2):
        put(sv.at[x2, z], rv.at[x, z], v1s.at[x2], v2r.at[x], slot=at(x2, z))

    give_row(FAR)
    loop(x + 1, NX, give)
    loop(x + 1, NX, give_k)
    for d in (1, 3, 2):
        x2 = (x + d) % NX
        put(wt.at[x2], wz.at[z, x], w1s.at[0], w1r.at[0], slot=at(x2, z))
    mine_w = pltpu.make_async_copy(wt.at[x], wz.at[z, x], ins.at[4])
    mine_w.start()

    def blank(z1):
        rk[x, z1] = jnp.zeros(rk.shape[2:], BF)
        rv[x, z1] = jnp.zeros(rv.shape[2:], BF)

    loop(z, NZ, blank)

    for copy in fetch:
        copy.wait()
    mine_w.wait()
    for h in range(heads):
        cols = slice(h * HD, (h + 1) * HD)
        s = lax.dot_general(q[:, cols], kn[:, cols], NT, preferred_element_type=F32)
        top = jnp.broadcast_to(jnp.max(s, 1, keepdims=True), (256, HD))
        p = jnp.exp2((s - jnp.concatenate([top, top], 1)) * c2)
        mx[h] = top
        tot[h] = jnp.broadcast_to(jnp.sum(p, 1, keepdims=True), (256, HD))
        acc[:, cols] = jnp.dot(p.astype(BF), vn[:, cols], preferred_element_type=F32)

    def chunk(x1):
        ok = seen[x1][0:1, :] > 0.5
        for h in range(heads):
            cols = slice(h * HD, (h + 1) * HD)
            keys = rk[x1, :, :, cols].reshape(256, HD)
            vals = rv[x1, :, :, cols].reshape(256, HD)
            s = lax.dot_general(q[:, cols], keys, NT, preferred_element_type=F32)
            s = jnp.where(ok, s, NEG)
            old = mx[h]
            top = jnp.maximum(old, jnp.max(s, 1, keepdims=True))
            fade = jnp.exp2((old - top) * c2)
            p = jnp.exp2((s - jnp.concatenate([top, top], 1)) * c2)
            mx[h] = top
            tot[h] = tot[h] * fade + jnp.sum(p, 1, keepdims=True)
            acc[:, cols] = acc[:, cols] * fade + jnp.dot(p.astype(BF), vals, preferred_element_type=F32)

    def w_pass(zs, sem):
        @pl.when(zs // 4 != core)
        def _():
            put(wz.at[zs], ws.at[zs % 4], wcs.at[0], wcr.at[zs % 4], tp=sib)

    def ring_step(k):
        zp, zm = (z + 1) % NZ, (z + NZ - 1) % NZ
        up, dn = (z + NZ - k + 1) % NZ, (z + k - 1) % NZ
        if k == 1:
            take(ws.at[0, pl.ds(0, 3)], w1r.at[0])
        if k > 1:
            take(wz.at[up], wpr.at[k - 2])
            take(wz.at[dn], wmr.at[k - 2])
        if k < 4:
            put(wz.at[up], wz.at[up], wps.at[0], wpr.at[k - 1], slot=at(x, zp))
            put(wz.at[dn], wz.at[dn], wms.at[0], wmr.at[k - 1], slot=at(x, zm))
        else:
            put(wz.at[up, pl.ds(0, 2)], wz.at[up, pl.ds(0, 2)], wps.at[1], wpr.at[3], slot=at(x, zp))
            put(wz.at[dn, pl.ds(2, 2)], wz.at[dn, pl.ds(2, 2)], wms.at[1], wmr.at[3], slot=at(x, zm))
        w_pass(up, 0)
        if k > 1:
            w_pass(dn, 0)

    def fwd_k(ds, i):
        x1 = x - 1 - i
        take(kb.at[x1, pl.ds(0, len(ds))], k1r.at[x1, 0 if ds is FAR else 1])
        for d in ds:
            z2 = (z + d) % NZ
            put(kb.at[x1, z2], rk.at[x1, z], k2s.at[x1], k2r.at[x1], slot=at(x, z2))

    give_row(NEAR)
    loop(x + 1, NX, functools.partial(give_v, NEAR))
    loop(x + 1, NX, give_rest)
    loop(0, x, functools.partial(fwd_k, FAR))
    loop(0, x, functools.partial(fwd_k, NEAR))

    def own_row(z1):
        take(vb.at[0, pl.ds(0, 2)], orr.at[z1])

    loop(0, z, own_row)
    chunk(x)

    for i, d in enumerate(FAR + NEAR):
        z2 = (z + d) % NZ

        def fwd_v(x2):
            take(vb.at[x2, z2], v1r.at[x2, z2])
            put(vb.at[x2, z2], rv.at[x, z2], v2s.at[x2], v2r.at[x], slot=at(x2, z))

        loop(x + 1, NX, fwd_v)
        if i == 2:
            ring_step(1)
    ring_step(2)

    def earlier(i):
        x1 = x - 1 - i
        take(rk.at[x1], k2r.at[x1])
        take(rv.at[x1], v2r.at[x1])
        chunk(x1)

    loop(0, x, earlier)
    for h in range(heads):
        cols = slice(h * HD, (h + 1) * HD)
        a[core, x, :, cols] = (acc[:, cols] / tot[h]).astype(BF)

    def rows(c, g, r):
        return a.at[c, g, pl.ds(r * 128, 128)]

    def to_sib(g, r):
        put(rows(core, g, r), rows(core, g, r), cs.at[0], cr.at[g, r], tp=sib)

    def from_sib(g, r):
        take(rows(1 - core, g, r), cr.at[g, r])

    for r in range(2):
        put(rows(core, x, r), rows(core, x, r), a1s.at[0], a1r.at[0, r], slot=at(right, z))
        put(rows(core, x, 1 - r), rows(core, x, 1 - r), a1s.at[0], a1r.at[1, 1 - r], slot=at(left, z))
    to_sib(x, 0)
    to_sib(x, 1)
    ring_step(3)

    def tile(g, zl, r, n):
        zs = core * 4 + zl
        o = lax.dot_general(wz[zs].reshape(192, 768), a[core, g, pl.ds(r * 128, n * 128)], NT, preferred_element_type=F32)
        o += lax.dot_general(ws[zl].reshape(192, 768), a[1 - core, g, pl.ds(r * 128, n * 128)], NT, preferred_element_type=F32)
        for i in range(n):
            for p in range(NY):
                part[g, r + i, p, zl] = o[p * 48 : (p + 1) * 48, i * 128 : (i + 1) * 128].astype(BF)
            for d in (2, 1, 3):
                p = (y + d) % NY
                put(
                    part.at[g, r + i, p, zl], got.at[g, r + i, y, zl],
                    ys.at[0], yr.at[g, r + i], tp=p * 2 + core,
                )

    def tiles(g, r, n, k0, k1):
        def one(k):
            d = (k % 2) * ((k + 1) // 2) + (1 - k % 2) * ((NZ - k // 2) % NZ)
            zs = (z + d) % NZ

            @pl.when(zs // 4 == core)
            def _():
                tile(g, zs % 4, r, n)

        loop(k0, k1, one)

    def w_here(k0, k1):
        def one(k):
            d = (k % 2) * ((k + 1) // 2) + (1 - k % 2) * ((NZ - k // 2) % NZ)
            zs = (z + d) % NZ

            @pl.when(zs // 4 == core)
            def _():
                take(ws.at[zs % 4], wcr.at[zs % 4])

        loop(k0, k1, one)

    def half_in(i):
        if i == 0:
            take(rows(core, left, 0), a1r.at[0, 0])
            put(rows(core, left, 0), rows(core, left, 0), a1s.at[0], a2r.at[0], slot=at(right, z))
            to_sib(left, 0)
            take(rows(core, right, 1), a1r.at[1, 1])
            put(rows(core, right, 1), rows(core, right, 1), a1s.at[0], a2r.at[1], slot=at(left, z))
            to_sib(right, 1)
        else:
            take(rows(core, left, 1), a1r.at[0, 1])
            to_sib(left, 1)
            take(rows(core, right, 0), a1r.at[1, 0])
            to_sib(right, 0)

    for r in range(2):
        from_sib(x, r)
    w_here(0, 3)
    tiles(x, 0, 2, 0, 3)
    half_in(0)
    w_here(3, 5)
    tiles(x, 0, 2, 3, 5)
    from_sib(left, 0)
    tiles(left, 0, 1, 0, 5)
    from_sib(right, 1)
    tiles(right, 1, 1, 0, 5)
    half_in(1)
    from_sib(left, 1)
    tiles(left, 1, 1, 0, 5)
    ring_step(4)
    from_sib(right, 0)
    tiles(right, 0, 1, 0, 5)
    w_here(5, 7)
    tiles(x, 0, 2, 5, 7)
    tiles(left, 0, 2, 5, 7)
    tiles(right, 0, 2, 5, 7)
    take(rows(core, across, 0), a2r.at[0])
    to_sib(across, 0)
    take(rows(core, across, 1), a2r.at[1])
    to_sib(across, 1)
    for r in range(2):
        from_sib(across, r)
    tiles(across, 0, 2, 0, 7)
    far = (z + 4) % NZ
    take(wz.at[far, pl.ds(0, 2)], wpr.at[3])
    take(wz.at[far, pl.ds(2, 2)], wmr.at[3])
    w_pass(far, 0)
    w_here(7, 8)
    for g in (across, left, right, x):
        tiles(g, 0, 2, 7, 8)

    def reduce(g, r):
        take(got.at[g, r, pl.ds(0, 3)], yr.at[g, r])
        s = part[g, r, y].astype(F32)
        for d in (1, 3, 2):
            src = (y + NY - d) % NY
            s += got[g, r, src].astype(F32)
        return s.astype(BF)

    for d in (3, 1, 2):
        g = (x + d) % NX
        for r in range(2):
            red[g, r] = reduce(g, r)
        put(red.at[g], fin.at[x], hs.at[0], hr.at[0], slot=at(g, z))
    for r in range(2):
        fin[x, r] = reduce(x, r)
    take(red.at[pl.ds(0, 3)], hr.at[0])
    for src in range(NX):
        for zs in range(4):
            for r in range(2):
                flat[zs * 192 + src * 48 : zs * 192 + (src + 1) * 48, r * 128 : (r + 1) * 128] = fin[src, r, zs]
    sub = lax.broadcasted_iota(jnp.int32, (256, 256), 0)
    lane = lax.broadcasted_iota(jnp.int32, (256, 256), 1)
    eye = jnp.where(sub == lane, 1.0, 0.0).astype(BF)
    summed = lax.dot_general(eye, flat[...], NT, preferred_element_type=F32)
    out[...] = (resid[...].astype(F32) + summed).astype(BF)

    sent(ws.at[0, pl.ds(0, 3)], w1s.at[0])
    sent(red.at[pl.ds(0, 3)], hs.at[0])
    sent(wz.at[pl.ds(0, 3)], wps.at[0])
    sent(wz.at[pl.ds(0, 3)], wms.at[0])
    sent(wz.at[z, pl.ds(0, 2)], wps.at[1])
    sent(wz.at[z, pl.ds(2, 2)], wms.at[1])
    sent(wz.at[pl.ds(0, 4)], wcs.at[0])
    sent(a.at[core], cs.at[0])
    sent(a.at[core, pl.ds(0, 3)], a1s.at[0])
    sent(part.at[:, :, pl.ds(0, 3)], ys.at[0])

    def row_sent(z2):
        sent(sk.at[x, pl.ds(0, 2)], os.at[z2])

    def given(x2):
        sent(sk.at[x2], k1s.at[x2])
        sent(sv.at[x2], v1s.at[x2])
        sent(vb.at[x2, pl.ds(0, NZ - 1)], v2s.at[x2])

    def passed(x1):
        sent(kb.at[x1, pl.ds(0, NZ - 1)], k2s.at[x1])

    loop(z + 1, NZ, row_sent)
    loop(x + 1, NX, given)
    loop(0, x, passed)


def per_device(queries, k_new, v_new, k_clean, v_clean, lists, counts, resid, w_out):
    width = queries.shape[1]
    wt = w_out.T.reshape(NX, 48, width)
    blocks = (-1, BLK, width)
    vm, hbm = pl.BlockSpec(memory_space=VM), pl.BlockSpec(memory_space=pl.ANY)
    heads = width // HD
    return pl.pallas_call(
        layer_kernel,
        out_shape=jax.ShapeDtypeStruct((256, width), BF),
        in_specs=[hbm] * 6 + [vm] * 2 + [hbm],
        out_specs=vm,
        scratch_shapes=[
            VM((256, width), BF), VM((256, width), BF), VM((256, width), BF), VM((256, width), BF),
            VM((256 // BLK, BLK, width), BF), VM((256 // BLK, BLK, width), BF), DMA((7,)),
            VM((NX, NZ, 32, width), BF), VM((NX, NZ, 32, width), BF),
            VM((NX, NZ, 32, width), BF), VM((NX, NZ, 32, width), BF),
            VM((NX, NZ, 32, width), BF), VM((NX, NZ, 32, width), BF),
            VM((NZ, NX, 48, width), BF), VM((4, NX, 48, width), BF), VM((NX, 8, 256), F32),
            VM((heads, 256, HD), F32), VM((heads, 256, HD), F32), VM((256, width), F32),
            VM((8, 128), jnp.int32), pltpu.SMEM((8, 128), jnp.int32),
            VM((2, NX, 256, width), BF), VM((NX, 2, NY, 4, 48, 128), BF), VM((NX, 2, NY, 4, 48, 128), BF),
            VM((NX, 2, 4, 48, 128), BF), VM((NX, 2, 4, 48, 128), BF), VM((width, 256), BF),
            DMA, DMA((NX,)), DMA((NX, 2)), DMA((NX,)), DMA((NX,)),
            DMA((NX,)), DMA((NX, NZ)), DMA((NX,)), DMA((NX,)),
            DMA((NZ,)), DMA((NZ,)), DMA((1,)), DMA((1,)),
            DMA((2,)), DMA((4,)), DMA((2,)), DMA((4,)), DMA((1,)), DMA((4,)),
            DMA((1,)), DMA((NX, 2)), DMA((1,)), DMA((2, 2)), DMA((1,)), DMA((2,)),
            DMA((1,)), DMA((NX, 2)), DMA((1,)), DMA((1,)),
        ],
        compiler_params=pltpu.CompilerParams(
            collective_id=0, has_side_effects=True, vmem_limit_bytes=56 << 20
        ),
        name="layer",
    )(
        queries, k_new, v_new, k_clean.reshape(blocks), v_clean.reshape(blocks), wt,
        lists, counts.reshape(1, -1), resid,
    )


def solution(mesh):
    in_specs = (
        P("slot", "tp"),
        P("slot", "tp"),
        P("slot", "tp"),
        P("slot", "tp"),
        P("slot", "tp"),
        P(),
        P(),
        P("slot", "tp"),
        P("tp", "slot"),
    )
    out_specs = P("slot", "tp")
    return jax.shard_map(
        per_device, mesh=mesh, in_specs=in_specs, out_specs=out_specs, check_vma=False
    )
```

```python
import functools
import math

import jax
import jax.numpy as jnp
from jax import lax
from jax.experimental import pallas as pl
from jax.experimental.pallas import tpu as pltpu
from jax.sharding import PartitionSpec as P

HD = 128
BLK = 16
NX, NZ, NY = 4, 8, 4
PAIR = {4: 0, 3: 1, 5: 1, 2: 2, 6: 2, 1: 3, 7: 3}
FAR, NEAR = (4, 3, 5), (2, 6, 1, 7)
MESH = pl.DeviceIdType.MESH
BF = jnp.bfloat16
F32 = jnp.float32
NEG = -1e30
NT = (((1,), (1,)), ((), ()))
VM = pltpu.VMEM
DMA = pltpu.SemaphoreType.DMA


def remote(src, dst, ssem, rsem, **where):
    return pltpu.make_async_remote_copy(
        src_ref=src, dst_ref=dst, send_sem=ssem, recv_sem=rsem, device_id=where, device_id_type=MESH
    )


def loop(lo, hi, body):
    def step(i, c):
        body(i)
        return c

    lax.fori_loop(lo, hi, step, 0)


def layer_kernel(
    q_in, kn_in, vn_in, kc_in, vc_in, wt, lists, counts, res_in,
    out,
    q, kn, vn, resid, kc, vc, ins,
    sk, sv, kb, vb, rk, rv, wz, ws, seen, mx, tot, acc, tab, tabs,
    a, part, got, red, fin, flat,
    ts, k1s, k1r, k2s, k2r, v1s, v1r, v2s, v2r, os, orr, w1s, w1r, wps, wpr, wms, wmr, wcs, wcr,
    cs, cr, a1s, a1r, a2s, a2r, ys, yr, hs, hr,
):
    me = lax.axis_index("slot")
    tp = lax.axis_index("tp")
    x, z, y, core = me // NZ, me % NZ, tp // 2, tp % 2
    sib = tp + 1 - 2 * core
    left, right, across = (x + 3) % NX, (x + 1) % NX, (x + 2) % NX
    heads = q.shape[1] // HD
    c2 = math.log2(math.e) / math.sqrt(HD)

    def at(ax, az):
        return ax * NZ + az

    def put(src, dst, ssem, rsem, **where):
        remote(src, dst, ssem, rsem, **where).start()

    def take(dst, rsem):
        remote(dst, dst, rsem, rsem, slot=me).wait_recv()

    def sent(src, ssem):
        remote(src, src, ssem, ssem, slot=me).wait_send()

    barrier = pltpu.get_barrier_semaphore()
    for d in range(1, NX):
        pl.semaphore_signal(barrier, inc=1, device_id={"slot": at((x + d) % NX, z)}, device_id_type=MESH)
    for d in range(1, NZ):
        pl.semaphore_signal(barrier, inc=1, device_id={"slot": at(x, (z + d) % NZ)}, device_id_type=MESH)
    for d in range(1, NY):
        pl.semaphore_signal(barrier, inc=1, device_id={"tp": ((y + d) % NY) * 2 + core}, device_id_type=MESH)
    pl.semaphore_signal(barrier, inc=1, device_id={"tp": sib}, device_id_type=MESH)

    blocks = [pltpu.make_async_copy(kc_in, kc, ins.at[5]), pltpu.make_async_copy(vc_in, vc, ins.at[6])]
    for copy in blocks:
        copy.start()
    fetch = [
        pltpu.make_async_copy(src, dst, ins.at[i])
        for i, (src, dst) in enumerate(((q_in, q), (kn_in, kn), (vn_in, vn), (res_in, resid)))
    ]
    for copy in fetch:
        copy.start()

    lst = lists[...]
    readers = lst.shape[0]
    sub = lax.broadcasted_iota(jnp.int32, (readers, 128), 0)
    lane = lax.broadcasted_iota(jnp.int32, (readers, 128), 1)
    live_n = jnp.sum(jnp.where(sub[:, :readers] == lane[:, :readers], counts[...], 0), 1, keepdims=True)
    live = lax.broadcasted_iota(jnp.int32, lst.shape, 1) < live_n
    mine = live & (lst // BLK == me)
    within = lst % BLK
    lo = jnp.min(jnp.where(mine, within, BLK), 1, keepdims=True)
    hi = jnp.max(jnp.where(mine, within, 0), 1, keepdims=True)
    lo = jnp.where(lo < BLK, lo, 0)
    tab[0:1, :] = jnp.sum(jnp.where(sub == lane, lo, 0), 0, keepdims=True)
    tab[1:2, :] = jnp.sum(jnp.where(sub == lane, hi, 0), 0, keepdims=True)
    to_scalar = pltpu.make_async_copy(tab, tabs, ts)
    to_scalar.start()

    row = lists[pl.ds(me, 1), :]
    n_live = jnp.sum(jnp.where(lax.broadcasted_iota(jnp.int32, counts.shape, 1) == me, counts[...], 0), 1, keepdims=True)
    row_live = lax.broadcasted_iota(jnp.int32, row.shape, 1) < n_live
    owner = lax.broadcasted_iota(jnp.int32, lst.shape, 0)
    n_of = jnp.sum(jnp.where((row // BLK == owner) & row_live, 1, 0), 1, keepdims=True)
    for x1 in range(NX):
        key = lax.broadcasted_iota(jnp.int32, (readers, 256), 1)
        own_of = lax.broadcasted_iota(jnp.int32, (readers, 256), 0)
        cnt = jnp.sum(jnp.where(own_of == x1 * NZ + key // 32, n_of, 0), 0, keepdims=True)
        odd = (lax.broadcasted_iota(jnp.int32, (1, 256), 1) // BLK) % 2
        seen[x1] = jnp.broadcast_to(jnp.where(cnt > odd, 1.0, 0.0), (8, 256))
    to_scalar.wait()

    def pack(x2):
        for z2 in range(NZ):
            r = at(x2, z2)
            for half in range(2):
                blk = tabs[half, r]
                sk[x2, z2, half * BLK : (half + 1) * BLK, :] = kc[blk]
                sv[x2, z2, half * BLK : (half + 1) * BLK, :] = vc[blk]

    for copy in blocks:
        copy.wait()
    pack(x)
    pl.semaphore_wait(barrier, NX - 1 + NZ - 1 + NY - 1 + 1)

    def give_row(ds):
        for d in ds:
            z2 = (z + d) % NZ

            @pl.when(z2 > z)
            def _():
                put(sk.at[x, z2], rk.at[x, z], os.at[z2], orr.at[z], slot=at(x, z2))
                put(sv.at[x, z2], rv.at[x, z], os.at[z2], orr.at[z], slot=at(x, z2))

    def give_v(ds, x2):
        for d in ds:
            z2 = (z + d) % NZ
            put(sv.at[x2, z2], vb.at[x2, z], v1s.at[x2], v1r.at[x2, PAIR[d]], slot=at(x, z2))

    def give(x2):
        pack(x2)
        for d in FAR:
            z2 = (z + d) % NZ
            put(sv.at[x2, z2], vb.at[x2, z], v1s.at[x2], v1r.at[x2, PAIR[d]], slot=at(x, z2))
            put(sk.at[x2, z2], kb.at[x, z2], k1s.at[x2], k1r.at[x, 0], slot=at(x2, z))

    def give_k(x2):
        for d in NEAR:
            z2 = (z + d) % NZ
            put(sk.at[x2, z2], kb.at[x, z2], k1s.at[x2], k1r.at[x, 1], slot=at(x2, z))
        put(sk.at[x2, z], rk.at[x, z], k1s.at[x2], k2r.at[x], slot=at(x2, z))

    def give_rest(x2):
        put(sv.at[x2, z], rv.at[x, z], v1s.at[x2], v2r.at[x], slot=at(x2, z))

    give_row(FAR)
    loop(x + 1, NX, give)
    loop(x + 1, NX, give_k)
    for d in (1, 3, 2):
        x2 = (x + d) % NX
        put(wt.at[x2], wz.at[z, x], w1s.at[0], w1r.at[0], slot=at(x2, z))
    mine_w = pltpu.make_async_copy(wt.at[x], wz.at[z, x], ins.at[4])
    mine_w.start()

    def blank(z1):
        rk[x, z1] = jnp.zeros(rk.shape[2:], BF)
        rv[x, z1] = jnp.zeros(rv.shape[2:], BF)

    loop(z, NZ, blank)

    for copy in fetch:
        copy.wait()
    mine_w.wait()
    for h in range(heads):
        cols = slice(h * HD, (h + 1) * HD)
        s = lax.dot_general(q[:, cols], kn[:, cols], NT, preferred_element_type=F32)
        top = jnp.broadcast_to(jnp.max(s, 1, keepdims=True), (256, HD))
        p = jnp.exp2((s - jnp.concatenate([top, top], 1)) * c2)
        mx[h] = top
        tot[h] = jnp.broadcast_to(jnp.sum(p, 1, keepdims=True), (256, HD))
        acc[:, cols] = jnp.dot(p.astype(BF), vn[:, cols], preferred_element_type=F32)

    def chunk(x1):
        ok = seen[x1][0:1, :] > 0.5
        for h in range(heads):
            cols = slice(h * HD, (h + 1) * HD)
            keys = rk[x1, :, :, cols].reshape(256, HD)
            vals = rv[x1, :, :, cols].reshape(256, HD)
            s = lax.dot_general(q[:, cols], keys, NT, preferred_element_type=F32)
            s = jnp.where(ok, s, NEG)
            old = mx[h]
            top = jnp.maximum(old, jnp.max(s, 1, keepdims=True))
            fade = jnp.exp2((old - top) * c2)
            p = jnp.exp2((s - jnp.concatenate([top, top], 1)) * c2)
            mx[h] = top
            tot[h] = tot[h] * fade + jnp.sum(p, 1, keepdims=True)
            acc[:, cols] = acc[:, cols] * fade + jnp.dot(p.astype(BF), vals, preferred_element_type=F32)

    def w_pass(zs, sem):
        @pl.when(zs // 4 != core)
        def _():
            put(wz.at[zs], ws.at[zs % 4], wcs.at[0], wcr.at[zs % 4], tp=sib)

    def ring_step(k):
        zp, zm = (z + 1) % NZ, (z + NZ - 1) % NZ
        up, dn = (z + NZ - k + 1) % NZ, (z + k - 1) % NZ
        if k == 1:
            take(ws.at[0, pl.ds(0, 3)], w1r.at[0])
        if k > 1:
            take(wz.at[up], wpr.at[k - 2])
            take(wz.at[dn], wmr.at[k - 2])
        if k < 4:
            put(wz.at[up], wz.at[up], wps.at[0], wpr.at[k - 1], slot=at(x, zp))
            put(wz.at[dn], wz.at[dn], wms.at[0], wmr.at[k - 1], slot=at(x, zm))
        else:
            put(wz.at[up, pl.ds(0, 2)], wz.at[up, pl.ds(0, 2)], wps.at[1], wpr.at[3], slot=at(x, zp))
            put(wz.at[dn, pl.ds(2, 2)], wz.at[dn, pl.ds(2, 2)], wms.at[1], wmr.at[3], slot=at(x, zm))
        w_pass(up, 0)
        if k > 1:
            w_pass(dn, 0)

    def fwd_k(ds, i):
        x1 = x - 1 - i
        take(kb.at[x1, pl.ds(0, len(ds))], k1r.at[x1, 0 if ds is FAR else 1])
        for d in ds:
            z2 = (z + d) % NZ
            put(kb.at[x1, z2], rk.at[x1, z], k2s.at[x1], k2r.at[x1], slot=at(x, z2))

    give_row(NEAR)
    loop(x + 1, NX, functools.partial(give_v, NEAR))
    loop(x + 1, NX, give_rest)
    loop(0, x, functools.partial(fwd_k, FAR))
    loop(0, x, functools.partial(fwd_k, NEAR))

    def own_row(z1):
        take(vb.at[0, pl.ds(0, 2)], orr.at[z1])

    loop(0, z, own_row)
    chunk(x)

    for i, d in enumerate(FAR + NEAR):
        z2 = (z + d) % NZ

        def fwd_v(x2):
            if d in (4, 3, 2, 1):
                take(vb.at[x2, pl.ds(0, 1 if d == 4 else 2)], v1r.at[x2, PAIR[d]])
            put(vb.at[x2, z2], rv.at[x, z2], v2s.at[x2], v2r.at[x], slot=at(x2, z))

        loop(x + 1, NX, fwd_v)
        if i == 2:
            ring_step(1)
    ring_step(2)

    def earlier(i):
        x1 = x - 1 - i
        take(rk.at[x1], k2r.at[x1])
        take(rv.at[x1], v2r.at[x1])
        chunk(x1)

    loop(0, x, earlier)
    for h in range(heads):
        cols = slice(h * HD, (h + 1) * HD)
        a[core, x, :, cols] = (acc[:, cols] / tot[h]).astype(BF)

    def rows(c, g, r):
        return a.at[c, g, pl.ds(r * 128, 128)]

    def to_sib(g, r):
        put(rows(core, g, r), rows(core, g, r), cs.at[0], cr.at[g, r], tp=sib)

    def from_sib(g, r):
        take(rows(1 - core, g, r), cr.at[g, r])

    for r in range(2):
        put(rows(core, x, r), rows(core, x, r), a1s.at[0], a1r.at[0, r], slot=at(right, z))
        put(rows(core, x, 1 - r), rows(core, x, 1 - r), a1s.at[0], a1r.at[1, 1 - r], slot=at(left, z))
    to_sib(x, 0)
    to_sib(x, 1)
    ring_step(3)

    def tile(g, zl, r, n):
        zs = core * 4 + zl
        o = lax.dot_general(wz[zs].reshape(192, 768), a[core, g, pl.ds(r * 128, n * 128)], NT, preferred_element_type=F32)
        o += lax.dot_general(ws[zl].reshape(192, 768), a[1 - core, g, pl.ds(r * 128, n * 128)], NT, preferred_element_type=F32)
        for i in range(n):
            for p in range(NY):
                part[g, r + i, p, zl] = o[p * 48 : (p + 1) * 48, i * 128 : (i + 1) * 128].astype(BF)
            for d in (2, 1, 3):
                p = (y + d) % NY
                put(
                    part.at[g, r + i, p, zl], got.at[g, r + i, y, zl],
                    ys.at[0], yr.at[g, r + i], tp=p * 2 + core,
                )

    def tiles(g, r, n, k0, k1):
        def one(k):
            d = (k % 2) * ((k + 1) // 2) + (1 - k % 2) * ((NZ - k // 2) % NZ)
            zs = (z + d) % NZ

            @pl.when(zs // 4 == core)
            def _():
                tile(g, zs % 4, r, n)

        loop(k0, k1, one)

    def w_here(k0, k1):
        def one(k):
            d = (k % 2) * ((k + 1) // 2) + (1 - k % 2) * ((NZ - k // 2) % NZ)
            zs = (z + d) % NZ

            @pl.when(zs // 4 == core)
            def _():
                take(ws.at[zs % 4], wcr.at[zs % 4])

        loop(k0, k1, one)

    def half_in(i):
        if i == 0:
            take(rows(core, left, 0), a1r.at[0, 0])
            put(rows(core, left, 0), rows(core, left, 0), a1s.at[0], a2r.at[0], slot=at(right, z))
            to_sib(left, 0)
            take(rows(core, right, 1), a1r.at[1, 1])
            put(rows(core, right, 1), rows(core, right, 1), a1s.at[0], a2r.at[1], slot=at(left, z))
            to_sib(right, 1)
        else:
            take(rows(core, left, 1), a1r.at[0, 1])
            to_sib(left, 1)
            take(rows(core, right, 0), a1r.at[1, 0])
            to_sib(right, 0)

    for r in range(2):
        from_sib(x, r)
    w_here(0, 3)
    tiles(x, 0, 2, 0, 3)
    half_in(0)
    w_here(3, 5)
    tiles(x, 0, 2, 3, 5)
    from_sib(left, 0)
    tiles(left, 0, 1, 0, 5)
    from_sib(right, 1)
    tiles(right, 1, 1, 0, 5)
    half_in(1)
    from_sib(left, 1)
    tiles(left, 1, 1, 0, 5)
    ring_step(4)
    from_sib(right, 0)
    tiles(right, 0, 1, 0, 5)
    w_here(5, 7)
    tiles(x, 0, 2, 5, 7)
    tiles(left, 0, 2, 5, 7)
    tiles(right, 0, 2, 5, 7)
    take(rows(core, across, 0), a2r.at[0])
    to_sib(across, 0)
    take(rows(core, across, 1), a2r.at[1])
    to_sib(across, 1)
    for r in range(2):
        from_sib(across, r)
    tiles(across, 0, 2, 0, 7)
    far = (z + 4) % NZ
    take(wz.at[far, pl.ds(0, 2)], wpr.at[3])
    take(wz.at[far, pl.ds(2, 2)], wmr.at[3])
    w_pass(far, 0)
    w_here(7, 8)
    for g in (across, left, right, x):
        tiles(g, 0, 2, 7, 8)

    def reduce(g, r):
        take(got.at[g, r, pl.ds(0, 3)], yr.at[g, r])
        s = part[g, r, y].astype(F32)
        for d in (1, 3, 2):
            src = (y + NY - d) % NY
            s += got[g, r, src].astype(F32)
        return s.astype(BF)

    for d in (3, 1, 2):
        g = (x + d) % NX
        for r in range(2):
            red[g, r] = reduce(g, r)
        put(red.at[g], fin.at[x], hs.at[0], hr.at[0], slot=at(g, z))
    for r in range(2):
        fin[x, r] = reduce(x, r)
    take(red.at[pl.ds(0, 3)], hr.at[0])
    for src in range(NX):
        for zs in range(4):
            for r in range(2):
                flat[zs * 192 + src * 48 : zs * 192 + (src + 1) * 48, r * 128 : (r + 1) * 128] = fin[src, r, zs]
    sub = lax.broadcasted_iota(jnp.int32, (256, 256), 0)
    lane = lax.broadcasted_iota(jnp.int32, (256, 256), 1)
    eye = jnp.where(sub == lane, 1.0, 0.0).astype(BF)
    summed = lax.dot_general(eye, flat[...], NT, preferred_element_type=F32)
    out[...] = (resid[...].astype(F32) + summed).astype(BF)

    sent(ws.at[0, pl.ds(0, 3)], w1s.at[0])
    sent(red.at[pl.ds(0, 3)], hs.at[0])
    sent(wz.at[pl.ds(0, 3)], wps.at[0])
    sent(wz.at[pl.ds(0, 3)], wms.at[0])
    sent(wz.at[z, pl.ds(0, 2)], wps.at[1])
    sent(wz.at[z, pl.ds(2, 2)], wms.at[1])
    sent(wz.at[pl.ds(0, 4)], wcs.at[0])
    sent(a.at[core], cs.at[0])
    sent(a.at[core, pl.ds(0, 3)], a1s.at[0])
    sent(part.at[:, :, pl.ds(0, 3)], ys.at[0])

    def row_sent(z2):
        sent(sk.at[x, pl.ds(0, 2)], os.at[z2])

    def given(x2):
        sent(sk.at[x2], k1s.at[x2])
        sent(sv.at[x2], v1s.at[x2])
        sent(vb.at[x2, pl.ds(0, NZ - 1)], v2s.at[x2])

    def passed(x1):
        sent(kb.at[x1, pl.ds(0, NZ - 1)], k2s.at[x1])

    loop(z + 1, NZ, row_sent)
    loop(x + 1, NX, given)
    loop(0, x, passed)


def per_device(queries, k_new, v_new, k_clean, v_clean, lists, counts, resid, w_out):
    width = queries.shape[1]
    wt = w_out.T.reshape(NX, 48, width)
    blocks = (-1, BLK, width)
    vm, hbm = pl.BlockSpec(memory_space=VM), pl.BlockSpec(memory_space=pl.ANY)
    heads = width // HD
    return pl.pallas_call(
        layer_kernel,
        out_shape=jax.ShapeDtypeStruct((256, width), BF),
        in_specs=[hbm] * 6 + [vm] * 2 + [hbm],
        out_specs=vm,
        scratch_shapes=[
            VM((256, width), BF), VM((256, width), BF), VM((256, width), BF), VM((256, width), BF),
            VM((256 // BLK, BLK, width), BF), VM((256 // BLK, BLK, width), BF), DMA((7,)),
            VM((NX, NZ, 32, width), BF), VM((NX, NZ, 32, width), BF),
            VM((NX, NZ, 32, width), BF), VM((NX, NZ, 32, width), BF),
            VM((NX, NZ, 32, width), BF), VM((NX, NZ, 32, width), BF),
            VM((NZ, NX, 48, width), BF), VM((4, NX, 48, width), BF), VM((NX, 8, 256), F32),
            VM((heads, 256, HD), F32), VM((heads, 256, HD), F32), VM((256, width), F32),
            VM((8, 128), jnp.int32), pltpu.SMEM((8, 128), jnp.int32),
            VM((2, NX, 256, width), BF), VM((NX, 2, NY, 4, 48, 128), BF), VM((NX, 2, NY, 4, 48, 128), BF),
            VM((NX, 2, 4, 48, 128), BF), VM((NX, 2, 4, 48, 128), BF), VM((width, 256), BF),
            DMA, DMA((NX,)), DMA((NX, 2)), DMA((NX,)), DMA((NX,)),
            DMA((NX,)), DMA((NX, 4)), DMA((NX,)), DMA((NX,)),
            DMA((NZ,)), DMA((NZ,)), DMA((1,)), DMA((1,)),
            DMA((2,)), DMA((4,)), DMA((2,)), DMA((4,)), DMA((1,)), DMA((4,)),
            DMA((1,)), DMA((NX, 2)), DMA((1,)), DMA((2, 2)), DMA((1,)), DMA((2,)),
            DMA((1,)), DMA((NX, 2)), DMA((1,)), DMA((1,)),
        ],
        compiler_params=pltpu.CompilerParams(
            collective_id=0, has_side_effects=True, vmem_limit_bytes=56 << 20
        ),
        name="layer",
    )(
        queries, k_new, v_new, k_clean.reshape(blocks), v_clean.reshape(blocks), wt,
        lists, counts.reshape(1, -1), resid,
    )


def solution(mesh):
    in_specs = (
        P("slot", "tp"),
        P("slot", "tp"),
        P("slot", "tp"),
        P("slot", "tp"),
        P("slot", "tp"),
        P(),
        P(),
        P("slot", "tp"),
        P("tp", "slot"),
    )
    out_specs = P("slot", "tp")
    return jax.shard_map(
        per_device, mesh=mesh, in_specs=in_specs, out_specs=out_specs, check_vma=False
    )
```
